32 devices in a mesh: grp: 2 (over core), gx: 4 (over z), gy: 4 (over y, x).
Axes of the slice: x: 2, y: 2, z: 4, core: 2. Of those that a mesh axis runs over, the one named last changes fastest.
Arguments:
- ocean_state: float32 [4, 60, 64, 512], P(None, None, ('grp', 'gx'), 'gy'), may hold values from -6 to 6
- diffusivity: float32 [64, 512], P(('grp', 'gx'), 'gy'), may hold values from 0.03 to 0.24
- wet_mask: int32 [64, 512], P(('grp', 'gx'), 'gy'), may hold values 0 or 1
- coast_column: int32 [8, 4, 32], P(('grp', 'gx'), 'gy'), may hold values from 0 to 1023, as said below
- coast_slot: int32 [8, 4, 32], P(('grp', 'gx'), 'gy'), may hold values from 0 to 63, as said below
- owner_node: int32 [8, 4, 16, 4], P(('grp', 'gx'), 'gy'), may hold values from -1 to 16383, as said below
- thickness: float32 [1024, 512], P(('grp', 'gx'), 'gy'), may hold values from 1 to 3
- viscosity: float32 [1024, 512], P(('grp', 'gx'), 'gy'), may hold values from 0.5 to 2
- friction: float32 [1024, 512], P(('grp', 'gx'), 'gy'), may hold values from 0.3 to 3
- grounded: int32 [1024, 512], P(('grp', 'gx'), 'gy'), may hold values 0 or 1
- coupling: float32 [1024, 512], P(('grp', 'gx'), 'gy'), may hold values from -1 to 1
- driving: float32 [2, 1024, 512], P(None, ('grp', 'gx'), 'gy'), may hold values from -16 to 16
- first_guess: float32 [2, 1024, 512], P(None, ('grp', 'gx'), 'gy'), may hold values from -2 to 2
Outputs:
- ocean_next: float32 [4, 60, 64, 512], P(None, None, ('grp', 'gx'), 'gy')
- melt_mean: float32 [64, 512], P(('grp', 'gx'), 'gy')
- velocity: float32 [2, 1024, 512], P(None, ('grp', 'gx'), 'gy')
- residual: float32 [2, 1024, 512], P(None, ('grp', 'gx'), 'gy')
The draws below stay inside these ranges and needn't reach their ends.
Inputs may be any that keep to these rules, and one draw needn't show every extreme that they name: `coast_column`: within a device the 32 numbers are distinct cells of its block. `coast_slot`: within a device the 32 slots are distinct, so at most 4 items go to one peer; every device sends 4 items to some peer. owner_node of an ice device at (peer p, s) is a node of its block exactly when peer p has an item with slot (this device's peer number) * 4 + s, else -1; the nodes of one device are distinct.
All inputs are finite; a program needn't handle non-finite values. No bound on the sum of `wet_mask` or of `grounded` on one device may be relied on, other than what follows from the above.
Results may differ from the reference program's by a relative error of at most 0.00012.
Values sent between devices are 32-bit elements; how exact they have to be, the bound alone decides.
A program may use at most 64 MiB of HBM per device.

```python
import math
import jax
import jax.numpy as jnp

LEV = 60
CX = 8
CY = 128
IX = 128
NSUB = 4
ITERS = 2
CAP = 4
XB = 8
YB = 4
PEERS = 16
G_DEV = 32
OX = 64
OY = 512
NXI = 1024
N_GX = 4
N_GY = 4


def coast_lists(key):
    base = jax.random.fold_in(key, 41)
    device_count = XB * YB
    slot_count = PEERS * CAP

    def one_device(device_key):
        key_order, key_full, key_cols, key_nodes = jax.random.split(device_key, 4)
        priority = jax.random.permutation(key_order, slot_count)
        full_peer = jax.random.randint(key_full, (), 0, PEERS)
        priority = jnp.where(jnp.arange(slot_count) // CAP == full_peer, priority - slot_count, priority)
        chosen = jnp.argsort(priority)[:G_DEV]
        columns = jax.random.permutation(key_cols, CX * CY)[:G_DEV]
        nodes = jax.random.permutation(key_nodes, IX * CY)[:slot_count]
        return (chosen.astype(jnp.int32), columns.astype(jnp.int32), nodes.astype(jnp.int32))
    chosen, columns, nodes = jax.vmap(one_device)(jax.random.split(base, device_count))
    used = jnp.zeros((device_count, slot_count), jnp.int32).at[jnp.arange(device_count)[:, None], chosen].set(1)
    halves = device_count // PEERS
    used = used.reshape(halves, PEERS, PEERS, CAP).transpose(0, 2, 1, 3).reshape(device_count, slot_count)
    owners = jnp.where(used == 1, nodes, -1).astype(jnp.int32)
    return (chosen.reshape(XB, YB, G_DEV), columns.reshape(XB, YB, G_DEV), owners.reshape(XB, YB, PEERS, CAP))


def draw_coast_slot(key, part):
    return coast_lists(key)[0]


def draw_coast_column(key, part):
    return coast_lists(key)[1]


def draw_owner_node(key, part):
    return coast_lists(key)[2]


def draw_driving(key, part):
    row_share = jnp.arange(NXI, dtype=jnp.float32) / max(NXI - 1, 1)
    rise_rows = 3.0 ** row_share
    noise = jnp.clip(jax.random.normal(key, (2, NXI, OY), jnp.float32), -4.0, 4.0)
    return noise * rise_rows[:, None]


def touch_ends(entries, key, least, high):
    dims = entries.shape
    place = [jax.random.randint(jax.random.fold_in(key, axis), (), 0, dims[axis]) for axis in range(len(dims))]
    entries = entries.at[tuple(place)].set(least)
    longest = dims.index(max(dims))
    place[longest] = (place[longest] + 1) % dims[longest]
    return entries.at[tuple(place)].set(high)


def shard_levels(key, shape, shards, least, top_value):
    gain = 1.0
    for axis_at, shards_of in shards:
        steps = jax.random.uniform(jax.random.fold_in(jax.random.fold_in(key, 6), axis_at), (shards_of,), jnp.float32, least / len(shards), top_value / len(shards))
        gain = gain * jnp.repeat(jnp.exp(steps), shape[axis_at] // shards_of).reshape((-1,) + (1,) * (len(shape) - 1 - axis_at))
    return gain


def centred(own_key, shape, width, reach, pieces=(), held_as=jnp.bfloat16):
    gain = shard_levels(own_key, shape, pieces, -0.22, 0.18) if pieces else 1.0
    drawn = jax.random.normal(own_key, shape, jnp.float32) * width * gain
    return jnp.minimum(jnp.maximum(drawn, -reach), reach).astype(held_as)


def setup_inputs(seed: int = 0) -> dict:
    key_list = jax.random.split(jax.random.key(seed), 14)
    ocean_state = centred(key_list[0], (4, LEV, OX, OY), 1.0, 6.0, ((2, 8), (3, 4)), jnp.float32)
    diffusivity = jnp.clip(jnp.exp(math.log(0.24) - 2.0794415 * jax.random.uniform(key_list[1], (OX, OY), jnp.float32) ** shard_levels(key_list[1], (OX, OY), ((0, 8), (1, 4)), -0.2, 0.2)), 0.03, 0.24)
    wet_mask = touch_ends((jax.random.randint(key_list[2], (OX, OY), 0, 8) < 7).astype(jnp.int32), jax.random.fold_in(key_list[2], 1), 0, 1)
    coast_column = draw_coast_column(jax.random.fold_in(key_list[13], 71), 0)
    coast_slot = draw_coast_slot(jax.random.fold_in(key_list[13], 71), 0)
    owner_node = draw_owner_node(jax.random.fold_in(key_list[13], 71), 0)
    thickness = jnp.clip(jnp.exp(math.log(3.0) - 1.0986123 * jax.random.uniform(key_list[6], (NXI, OY), jnp.float32) ** shard_levels(key_list[6], (NXI, OY), ((0, 8), (1, 4)), -0.2, 0.2)), 1.0, 3.0)
    viscosity = jnp.clip(jnp.exp(math.log(2.0) - 1.3862944 * jax.random.uniform(key_list[7], (NXI, OY), jnp.float32) ** shard_levels(key_list[7], (NXI, OY), ((0, 8), (1, 4)), -0.2, 0.2)), 0.5, 2.0)
    friction = jnp.clip(jnp.exp(math.log(3.0) - 2.3025851 * jax.random.uniform(key_list[8], (NXI, OY), jnp.float32) ** shard_levels(key_list[8], (NXI, OY), ((0, 8), (1, 4)), -0.2, 0.2)), 0.3, 3.0)
    grounded = touch_ends((jax.random.randint(key_list[9], (NXI, OY), 0, 2) < 1).astype(jnp.int32), jax.random.fold_in(key_list[9], 1), 0, 1)
    coupling = jnp.clip(jax.random.uniform(key_list[10], (NXI, OY), jnp.float32, -1.0, 1.0) * shard_levels(key_list[10], (NXI, OY), ((0, 8), (1, 4)), -0.4, 0.0), -1.0, 1.0)
    driving = draw_driving(jax.random.fold_in(key_list[13], 71), 0)
    first_guess = centred(key_list[12], (2, NXI, OY), 0.3, 2.0, ((1, 8), (2, 4)), jnp.float32)
    return {"ocean_state": ocean_state, "diffusivity": diffusivity, "wet_mask": wet_mask, "coast_column": coast_column, "coast_slot": coast_slot, "owner_node": owner_node, "thickness": thickness, "viscosity": viscosity, "friction": friction, "grounded": grounded, "coupling": coupling, "driving": driving, "first_guess": first_guess}


def advance(padded, diff_pad, wet_pad, cover, draft_field):
    fields = padded[:, :, 1:-1, 1:-1]
    row_total = fields.shape[2]
    col_total = fields.shape[3]
    diff_here = diff_pad[1:-1, 1:-1]
    wet_here = wet_pad[1:-1, 1:-1]
    flux_sum = jnp.zeros_like(fields)
    for offset in ((2, 1), (0, 1), (1, 2), (1, 0)):
        diff_side = diff_pad[offset[0]:offset[0] + row_total, offset[1]:offset[1] + col_total]
        wet_side = wet_pad[offset[0]:offset[0] + row_total, offset[1]:offset[1] + col_total]
        side_vals = padded[:, :, offset[0]:offset[0] + row_total, offset[1]:offset[1] + col_total]
        weight = 0.5 * (diff_here + diff_side) * wet_here * wet_side
        flux_sum = flux_sum + weight * (side_vals - fields)
    top_temp = fields[0, 0]
    top_salt = fields[1, 0]
    top_east = fields[2, 0]
    top_north = fields[3, 0]
    current_speed = jnp.sqrt(top_east * top_east + top_north * top_north + 0.01)
    freezing = -0.5 * top_salt + 0.3 * draft_field - 0.2
    melt_rate = 0.5 * cover * (top_temp - freezing) * current_speed
    updated = fields + flux_sum
    drag_rate = 0.05 * cover * current_speed
    top_rows = jnp.stack([updated[0, 0] - 0.3 * melt_rate, updated[1, 0] - 0.2 * melt_rate, updated[2, 0] - drag_rate * top_east, updated[3, 0] - drag_rate * top_north])
    updated = updated.at[:, 0].set(top_rows)
    return (updated, melt_rate)

def operator_parts(depth_visc, visc_pad, friction, grounded, coupling):
    weight_east = 0.5 * (depth_visc + visc_pad[2:, 1:-1])
    weight_west = 0.5 * (depth_visc + visc_pad[:-2, 1:-1])
    weight_north = 0.5 * (depth_visc + visc_pad[1:-1, 2:])
    weight_south = 0.5 * (depth_visc + visc_pad[1:-1, :-2])
    base_friction = friction * grounded.astype(jnp.float32) + 0.2
    cross_term = 0.9 * base_friction * coupling
    diagonal = weight_east + weight_west + weight_north + weight_south + base_friction
    return (diagonal, weight_east, weight_west, weight_north, weight_south, cross_term)

def apply_padded(vector_pad, parts):
    diagonal, weight_east, weight_west, weight_north, weight_south, cross_term = parts
    inner = vector_pad[:, 1:-1, 1:-1]
    beside = weight_east * vector_pad[:, 2:, 1:-1] + weight_west * vector_pad[:, :-2, 1:-1]
    beside = beside + weight_north * vector_pad[:, 1:-1, 2:] + weight_south * vector_pad[:, 1:-1, :-2]
    return diagonal * inner - beside + cross_term * inner[::-1]

def pad_vector(vector):
    return jnp.pad(vector, ((0, 0), (1, 1), (1, 1)))

def to_blocks(grid_field, row_count):
    return grid_field.reshape(XB, row_count, YB, CY).transpose(0, 2, 1, 3).reshape(XB, YB, row_count * CY)

def from_blocks(blocks, row_count):
    return blocks.reshape(XB, YB, row_count, CY).transpose(0, 2, 1, 3).reshape(XB * row_count, YB * CY)

def reference(ocean_state, diffusivity, wet_mask, coast_column, coast_slot, owner_node, thickness, viscosity, friction, grounded, coupling, driving, first_guess):
    block_x = jnp.broadcast_to(jnp.arange(XB, dtype=jnp.int32)[:, None, None], coast_slot.shape)
    block_y = jnp.broadcast_to(jnp.arange(YB, dtype=jnp.int32)[None, :, None], coast_slot.shape)
    peer_index = coast_slot // CAP
    slot_index = coast_slot % CAP
    owner_x = block_x // N_GX * N_GX + peer_index // N_GY
    owner_y = peer_index % N_GY
    sender = block_x % N_GX * N_GY + block_y
    node_index = owner_node[owner_x, owner_y, sender, slot_index]
    thick_blocks = to_blocks(thickness, IX)
    draft_item = 0.9 * thick_blocks[owner_x, owner_y, node_index]
    cover_blocks = jnp.zeros((XB, YB, CX * CY), jnp.float32).at[block_x, block_y, coast_column].set(1.0)
    draft_blocks = jnp.zeros((XB, YB, CX * CY), jnp.float32).at[block_x, block_y, coast_column].set(draft_item)
    cover = from_blocks(cover_blocks, CX)
    draft_field = from_blocks(draft_blocks, CX)
    diff_pad = jnp.pad(diffusivity, 1)
    wet_pad = jnp.pad(wet_mask.astype(jnp.float32), 1)
    fields = ocean_state
    total = jnp.zeros((OX, OY), jnp.float32)
    for substep in range(NSUB):
        padded = jnp.pad(fields, ((0, 0), (0, 0), (1, 1), (1, 1)))
        fields, melt_rate = advance(padded, diff_pad, wet_pad, cover, draft_field)
        total = total + melt_rate
    melt_mean = total / NSUB
    melt_item = to_blocks(melt_mean, CX)[block_x, block_y, coast_column]
    melt_node = jnp.zeros((XB, YB, IX * CY), jnp.float32).at[owner_x, owner_y, node_index].add(melt_item)
    thinned = thickness * jnp.exp(-0.3 * from_blocks(melt_node, IX))
    depth_visc = viscosity * thinned
    parts = operator_parts(depth_visc, jnp.pad(depth_visc, 1), friction, grounded, coupling)
    rhs = driving * thinned
    velocity = first_guess
    residual = rhs - apply_padded(pad_vector(first_guess), parts)
    precond = residual / parts[0]
    direction = precond
    norm_now = jnp.sum(residual * precond)
    for iteration in range(ITERS):
        image = apply_padded(pad_vector(direction), parts)
        step_size = norm_now / jnp.sum(direction * image)
        velocity = velocity + step_size * direction
        residual = residual - step_size * image
        if iteration + 1 < ITERS:
            precond = residual / parts[0]
            norm_next = jnp.sum(residual * precond)
            direction = precond + norm_next / norm_now * direction
            norm_now = norm_next
    return (fields, melt_mean, velocity, residual)
```

```python
import jax
import jax.numpy as jnp
from jax import lax
from jax.experimental import pallas as pl
from jax.experimental.pallas import tpu as pltpu
from jax.sharding import PartitionSpec as P

NSUB = 4
CAP = 4
MESH = pl.DeviceIdType.MESH


def padded_2(block, sides, width):
    for axis, dim in sides:
        count = lax.axis_size(axis)
        forward = [(i, i + 1) for i in range(count - 1)]
        backward = [(target, source) for source, target in forward]
        low = lax.ppermute(
            lax.slice_in_dim(block, block.shape[dim] - width, None, axis=dim), axis, forward
        )
        high = lax.ppermute(lax.slice_in_dim(block, 0, width, axis=dim), axis, backward)
        block = jnp.concatenate([low, block, high], axis=dim)
    return block


def advance(padded, diff_pad, wet_pad, cover, draft_field):
    fields = padded[:, :, 1:-1, 1:-1]
    row_total = fields.shape[2]
    col_total = fields.shape[3]
    diff_here = diff_pad[1:-1, 1:-1]
    wet_here = wet_pad[1:-1, 1:-1]
    flux_sum = jnp.zeros_like(fields)
    for offset in ((2, 1), (0, 1), (1, 2), (1, 0)):
        diff_side = diff_pad[offset[0] : offset[0] + row_total, offset[1] : offset[1] + col_total]
        wet_side = wet_pad[offset[0] : offset[0] + row_total, offset[1] : offset[1] + col_total]
        side_vals = padded[
            :, :, offset[0] : offset[0] + row_total, offset[1] : offset[1] + col_total
        ]
        weight = 0.5 * (diff_here + diff_side) * wet_here * wet_side
        flux_sum = flux_sum + weight * (side_vals - fields)
    top_temp = fields[0, 0]
    top_salt = fields[1, 0]
    top_east = fields[2, 0]
    top_north = fields[3, 0]
    current_speed = jnp.sqrt(top_east * top_east + top_north * top_north + 0.01)
    freezing = -0.5 * top_salt + 0.3 * draft_field - 0.2
    melt_rate = 0.5 * cover * (top_temp - freezing) * current_speed
    updated = fields + flux_sum
    drag_rate = 0.05 * cover * current_speed
    top_rows = jnp.stack(
        [
            updated[0, 0] - 0.3 * melt_rate,
            updated[1, 0] - 0.2 * melt_rate,
            updated[2, 0] - drag_rate * top_east,
            updated[3, 0] - drag_rate * top_north,
        ]
    )
    updated = updated.at[:, 0].set(top_rows)
    return (updated, melt_rate)


def device_tools(names):
    sizes = {name: lax.axis_size(name) for name in names}
    n_grp, n_gx, n_gy = sizes["grp"], sizes["gx"], sizes["gy"]
    grp, gx, gy = lax.axis_index("grp"), lax.axis_index("gx"), lax.axis_index("gy")
    bx = grp * n_gx + gx

    def at_row(row):
        return (row // n_gx, row % n_gx, gy)

    sides = (
        (bx > 0, at_row(jnp.maximum(bx - 1, 0))),
        (bx < n_grp * n_gx - 1, at_row(jnp.minimum(bx + 1, n_grp * n_gx - 1))),
        (gy > 0, (grp, gx, jnp.maximum(gy - 1, 0))),
        (gy < n_gy - 1, (grp, gx, jnp.minimum(gy + 1, n_gy - 1))),
    )
    return grp, gx, gy, n_grp, n_gx, n_gy, sides


def signal(semaphore, target):
    pl.semaphore_signal(semaphore, inc=1, device_id=target, device_id_type=MESH)


def enter(tools):
    grp, gx, gy, n_grp, n_gx, n_gy, sides = tools
    peers = n_gx * n_gy
    me = gx * n_gy + gy
    barrier = pltpu.get_barrier_semaphore()

    def greet(i, carry):
        peer = lax.rem(me + i, peers)
        signal(barrier, (grp, peer // n_gy, peer % n_gy))
        return carry

    lax.fori_loop(1, peers, greet, 0)
    for i in range(1, n_grp):
        signal(barrier, (lax.rem(grp + i, n_grp), gx, gy))
    cross_low = jnp.logical_and(gx == 0, grp > 0)
    cross_high = jnp.logical_and(gx == n_gx - 1, grp < n_grp - 1)

    @pl.when(cross_low)
    def _():
        signal(barrier, sides[0][1])

    @pl.when(cross_high)
    def _():
        signal(barrier, sides[1][1])

    extra = cross_low.astype(jnp.int32) + cross_high.astype(jnp.int32)
    pl.semaphore_wait(barrier, peers - 1 + n_grp - 1 + extra)


class Gather:
    def __init__(self, tools, source, rows, send_sems, recv_sems):
        self.tools, self.source, self.rows = tools, source, rows
        self.send_sems, self.recv_sems = send_sems, recv_sems
        self.peers = tools[4] * tools[5]
        self.me = tools[1] * tools[5] + tools[2]

    def copy(self, peer, slot):
        n_gy = self.tools[5]
        return pltpu.make_async_remote_copy(
            src_ref=self.source,
            dst_ref=self.rows.at[slot],
            send_sem=self.send_sems.at[peer],
            recv_sem=self.recv_sems.at[slot],
            device_id=(self.tools[0], peer // n_gy, peer % n_gy),
            device_id_type=MESH,
        )

    def start(self, block):
        self.source[...] = block
        self.rows[self.me] = block

        def step(i, carry):
            self.copy(lax.rem(self.me + i, self.peers), self.me).start()
            return carry

        lax.fori_loop(1, self.peers, step, 0)

    def wait(self):
        def step(i, carry):
            peer = lax.rem(self.me + i, self.peers)
            self.copy(peer, peer).wait_recv()
            return carry

        lax.fori_loop(1, self.peers, step, 0)

    def finish(self):
        def step(i, carry):
            peer = lax.rem(self.me + i, self.peers)
            self.copy(peer, peer).wait_send()
            return carry

        lax.fori_loop(1, self.peers, step, 0)


class Rim:
    def __init__(self, tools, source, landing, send_sems, recv_sems):
        self.sides = tools[6]
        self.source, self.landing = source, landing
        self.send_sems, self.recv_sems = send_sems, recv_sems

    def copy(self, side, slot):
        return pltpu.make_async_remote_copy(
            src_ref=self.source.at[side],
            dst_ref=self.landing.at[slot],
            send_sem=self.send_sems.at[side],
            recv_sem=self.recv_sems.at[slot],
            device_id=self.sides[side][1],
            device_id_type=MESH,
        )

    def start(self, side):
        @pl.when(self.sides[side][0])
        def _():
            self.copy(side, side ^ 1).start()

    def wait(self, side):
        @pl.when(self.sides[side][0])
        def _():
            self.copy(side, side).wait_recv()

        @pl.when(jnp.logical_not(self.sides[side][0]))
        def _():
            self.landing[side] = jnp.zeros_like(self.landing[side])

    def finish(self):
        for side in range(4):
            @pl.when(self.sides[side][0])
            def _():
                self.copy(side, side).wait_send()


def stack_rows(rows):
    width = rows[0].shape[1]
    place = lax.broadcasted_iota(jnp.int32, (8, width), 0)
    out = jnp.zeros((8, width), jnp.float32)
    for i, row in enumerate(rows):
        out = jnp.where(place == i, row, out)
    return out


def send_edges(rim, fields):
    last, right = fields[0].shape[0] - 1, fields[0].shape[1] - 1
    rim.source[0] = stack_rows([f[0:1] for f in fields])
    rim.start(0)
    rim.source[1] = stack_rows([f[last:] for f in fields])
    rim.start(1)
    turned = [f.T for f in fields]
    rim.source[2] = stack_rows([f[0:1] for f in turned])
    rim.start(2)
    rim.source[3] = stack_rows([f[right:] for f in turned])
    rim.start(3)


def rim_values(rim, count, shape):
    for side in range(4):
        rim.wait(side)
    row_count, col_count = shape
    line = lax.broadcasted_iota(jnp.int32, (col_count, row_count), 0)
    result = []
    for i in range(count):
        low, high = rim.landing[0, i : i + 1], rim.landing[1, i : i + 1]
        west, east = rim.landing[2, i : i + 1], rim.landing[3, i : i + 1]
        side = jnp.where(line == 0, west, jnp.where(line == col_count - 1, east, 0.0)).T
        result.append((low, high, side))
    return result


def around(field, rim):
    low, high, side = rim
    row_count, col_count = field.shape
    row = lax.broadcasted_iota(jnp.int32, field.shape, 0)
    col = lax.broadcasted_iota(jnp.int32, field.shape, 1)
    return (
        jnp.where(row == row_count - 1, high, pltpu.roll(field, row_count - 1, 0)),
        jnp.where(row == 0, low, pltpu.roll(field, 1, 0)),
        jnp.where(col == col_count - 1, side, pltpu.roll(field, col_count - 1, 1)),
        jnp.where(col == 0, side, pltpu.roll(field, 1, 1)),
    )


def ice_kernel(
    melt_ref,
    node_ref,
    thick_ref,
    visc_ref,
    fric_ref,
    ground_ref,
    coup_ref,
    drive_ref,
    guess_ref,
    vel_ref,
    res_ref,
    melt_src,
    melt_rows,
    sum_src,
    sum_rows,
    half_src,
    half_rows,
    edge_src,
    edge_land,
    melt_send,
    melt_recv,
    sum_send,
    sum_recv,
    half_send,
    half_recv,
    edge_send,
    edge_recv,
):
    tools = device_tools(("grp", "gx", "gy"))
    grp, gx, gy, n_grp, n_gx, n_gy, sides = tools
    enter(tools)
    me = gx * n_gy + gy
    peers = n_gx * n_gy
    gather = Gather(tools, melt_src, melt_rows, melt_send, melt_recv)
    gather.start(melt_ref[...])
    shape = thick_ref.shape
    width = melt_ref.shape[1]
    node = node_ref[...]
    friction = fric_ref[...] * ground_ref[...].astype(jnp.float32) + 0.2
    cross = 0.9 * friction * coup_ref[...]
    lane = lax.broadcasted_iota(jnp.int32, (1, width), 1)
    row_of = (lax.broadcasted_iota(jnp.int32, (shape[0], width), 0) == jnp.where(node < 0, -1, node // shape[1])).astype(jnp.float32)
    col_of = (lax.broadcasted_iota(jnp.int32, (shape[1], width), 0) == node % shape[1]).astype(jnp.float32)
    gather.wait()
    melt = jnp.zeros((1, width), jnp.float32)
    for p in range(peers):
        turn = lax.rem(CAP * (p - me) + width, width)
        melt = jnp.where(lane // CAP == p, pltpu.roll(melt_rows[p], turn, 1), melt)
    melt_node = lax.dot_general(
        row_of * melt, col_of, (((1,), (1,)), ((), ())),
        precision=lax.Precision.HIGHEST, preferred_element_type=jnp.float32,
    )
    thinned = thick_ref[...] * jnp.exp(-0.3 * melt_node)
    depth_visc = visc_ref[...] * thinned
    guess = [guess_ref[0], guess_ref[1]]
    rims = [Rim(tools, edge_src.at[e], edge_land.at[e], edge_send.at[e], edge_recv.at[e]) for e in range(3)]
    send_edges(rims[0], [depth_visc] + guess)
    values = rim_values(rims[0], 3, shape)
    weights = [0.5 * (depth_visc + beside) for beside in around(depth_visc, values[0])]
    diagonal = weights[0] + weights[1] + weights[2] + weights[3] + friction
    scale = 1.0 / diagonal

    def apply(vector, rim):
        out = []
        for i in range(2):
            beside = 0.0
            for weight, side in zip(weights, around(vector[i], rim[i])):
                beside = beside + weight * side
            out.append(diagonal * vector[i] - beside + cross * vector[1 - i])
        return out

    def half_sums(index, products):
        rows = [jnp.sum(a[0] * b[0] + a[1] * b[1], axis=0, keepdims=True) for a, b in products]
        part = Gather(tools, sum_src.at[index], sum_rows.at[index], sum_send.at[index], sum_recv.at[index])
        part.start(stack_rows(rows))
        return part

    def whole_sums(index, part, count):
        part.wait()
        total = jnp.sum(sum_rows[index], axis=0)
        half_src[index] = total
        copies = []
        for i in range(1, n_grp):
            copies.append(pltpu.make_async_remote_copy(
                src_ref=half_src.at[index], dst_ref=half_rows.at[index, i - 1],
                send_sem=half_send.at[index, i - 1], recv_sem=half_recv.at[index, i - 1],
                device_id=(lax.rem(grp + i, n_grp), gx, gy), device_id_type=MESH,
            ))
            copies[-1].start()
        for i, copy in enumerate(copies):
            copy.wait()
            total = total + half_rows[index, i]
        summed = jnp.sum(total, axis=1, keepdims=True)
        return [summed[i : i + 1] for i in range(count)]

    image = apply(guess, values[1:])
    residual = [drive_ref[i] * thinned - image[i] for i in range(2)]
    precond = [residual[i] * scale for i in range(2)]
    send_edges(rims[1], precond)
    edge_z = rim_values(rims[1], 2, shape)
    image = apply(precond, edge_z)
    scaled = [image[i] * scale for i in range(2)]
    part = half_sums(0, [(residual, precond), (precond, image)])
    send_edges(rims[2], scaled)
    edge_y = rim_values(rims[2], 2, shape)
    norm, curve = whole_sums(0, part, 2)
    step = norm / curve
    velocity = [guess[i] + step * precond[i] for i in range(2)]
    residual = [residual[i] - step * image[i] for i in range(2)]
    next_precond = [residual[i] * scale for i in range(2)]
    edge = [tuple(z - step * y for z, y in zip(edge_z[i], edge_y[i])) for i in range(2)]
    next_image = apply(next_precond, edge)
    second = half_sums(1, [(residual, next_precond), (next_precond, next_image), (next_precond, image)])
    norm_next, own_curve, mixed = whole_sums(1, second, 3)
    ratio = norm_next / norm
    step = norm_next / (own_curve + 2.0 * ratio * mixed + ratio * ratio * curve)
    for i in range(2):
        vel_ref[i] = velocity[i] + step * (next_precond[i] + ratio * precond[i])
        res_ref[i] = residual[i] - step * (next_image[i] + ratio * image[i])
    gather.finish()
    part.finish()
    second.finish()
    for rim in rims:
        rim.finish()


def ice_phase(melt_row, node_row, thickness, viscosity, friction, grounded, coupling, driving, first_guess):
    n_grp, n_gx, n_gy = lax.axis_size("grp"), lax.axis_size("gx"), lax.axis_size("gy")
    peers = n_gx * n_gy
    width = melt_row.shape[1]
    cols = thickness.shape[1]
    vmem = pl.BlockSpec(memory_space=pltpu.VMEM)
    dma = pltpu.SemaphoreType.DMA
    f32 = jnp.float32
    return pl.pallas_call(
        ice_kernel,
        out_shape=[jax.ShapeDtypeStruct(first_guess.shape, f32)] * 2,
        in_specs=[vmem] * 9,
        out_specs=[vmem] * 2,
        scratch_shapes=[
            pltpu.VMEM((1, width), f32),
            pltpu.VMEM((peers, 1, width), f32),
            pltpu.VMEM((2, 8, cols), f32),
            pltpu.VMEM((2, peers, 8, cols), f32),
            pltpu.VMEM((2, 8, cols), f32),
            pltpu.VMEM((2, n_grp - 1, 8, cols), f32),
            pltpu.VMEM((3, 4, 8, cols), f32),
            pltpu.VMEM((3, 4, 8, cols), f32),
            dma((peers,)),
            dma((peers,)),
            dma((2, peers)),
            dma((2, peers)),
            dma((2, n_grp - 1)),
            dma((2, n_grp - 1)),
            dma((3, 4)),
            dma((3, 4)),
        ],
        compiler_params=pltpu.CompilerParams(
            collective_id=0, has_side_effects=True, vmem_limit_bytes=32 * 1024 * 1024
        ),
    )(melt_row, node_row, thickness, viscosity, friction, grounded, coupling, driving, first_guess)


def shards(
    ocean_state,
    diffusivity,
    wet_mask,
    coast_column,
    coast_slot,
    owner_node,
    thickness,
    viscosity,
    friction,
    grounded,
    coupling,
    driving,
    first_guess,
):
    field_count, level_count, row_count, col_count = ocean_state.shape
    layers = field_count * level_count
    owner = owner_node[0, 0]
    valid = owner >= 0
    safe_node = jnp.where(valid, owner, 0)
    thick_flat = thickness.reshape(-1)
    draft_send = jnp.where(valid, 0.9 * thick_flat[safe_node], 0.0)
    draft_recv = lax.all_to_all(draft_send, ("gx", "gy"), split_axis=0, concat_axis=0, tiled=True)
    columns = coast_column[0, 0]
    slots = coast_slot[0, 0]
    draft_item = draft_recv.reshape(-1)[slots]
    cell_count = row_count * col_count
    cover = jnp.zeros((cell_count,), jnp.float32).at[columns].set(1.0).reshape(row_count, col_count)
    draft_field = (
        jnp.zeros((cell_count,), jnp.float32)
        .at[columns]
        .set(draft_item)
        .reshape(row_count, col_count)
    )
    wet_field = wet_mask.astype(jnp.float32)
    total = jnp.zeros((row_count, col_count), jnp.float32)
    fields = ocean_state
    stacked = jnp.concatenate(
        [
            fields.reshape(layers, row_count, col_count),
            diffusivity[None],
            wet_field[None],
            cover[None],
            draft_field[None],
        ],
        0,
    )
    padded = padded_2(stacked, ((("grp", "gx"), 1), ("gy", 2)), NSUB)
    current = padded[:layers].reshape(
        field_count, level_count, row_count + 2 * NSUB, col_count + 2 * NSUB
    )
    for substep in range(NSUB):
        stop_row = row_count + 2 * NSUB - substep
        stop_col = col_count + 2 * NSUB - substep
        diff_part = padded[layers, substep:stop_row, substep:stop_col]
        wet_part = padded[layers + 1, substep:stop_row, substep:stop_col]
        cover_part = padded[layers + 2, substep + 1 : stop_row - 1, substep + 1 : stop_col - 1]
        draft_part = padded[layers + 3, substep + 1 : stop_row - 1, substep + 1 : stop_col - 1]
        current, melt_rate = advance(current, diff_part, wet_part, cover_part, draft_part)
        margin = NSUB - substep - 1
        total = total + melt_rate[margin : margin + row_count, margin : margin + col_count]
    fields = current
    melt_mean = total / NSUB
    lanes = 128 * (-(-owner.size // 128))
    cells = jnp.arange(cell_count, dtype=jnp.int32)
    melt_item = jnp.sum(
        jnp.where(columns[:, None] == cells[None, :], melt_mean.reshape(1, -1), 0.0), axis=1
    )
    melt_row = jnp.sum(
        jnp.where(
            slots[:, None] == jnp.arange(lanes, dtype=jnp.int32)[None, :], melt_item[:, None], 0.0
        ),
        axis=0,
    )[None]
    node_row = jnp.pad(owner.reshape(1, -1), ((0, 0), (0, lanes - owner.size)), constant_values=-1)
    velocity, residual = ice_phase(
        melt_row, node_row, thickness, viscosity, friction, grounded, coupling, driving, first_guess
    )
    return (fields, melt_mean, velocity, residual)


def solution(mesh):
    in_specs = (
        P(None, None, ("grp", "gx"), "gy"),
        P(("grp", "gx"), "gy"),
        P(("grp", "gx"), "gy"),
        P(("grp", "gx"), "gy", None),
        P(("grp", "gx"), "gy", None),
        P(("grp", "gx"), "gy", None, None),
        P(("grp", "gx"), "gy"),
        P(("grp", "gx"), "gy"),
        P(("grp", "gx"), "gy"),
        P(("grp", "gx"), "gy"),
        P(("grp", "gx"), "gy"),
        P(None, ("grp", "gx"), "gy"),
        P(None, ("grp", "gx"), "gy"),
    )
    out_specs = (
        P(None, None, ("grp", "gx"), "gy"),
        P(("grp", "gx"), "gy"),
        P(None, ("grp", "gx"), "gy"),
        P(None, ("grp", "gx"), "gy"),
    )
    return jax.shard_map(shards, mesh=mesh, in_specs=in_specs, out_specs=out_specs, check_vma=False)
```

```python
import functools

import jax
import jax.numpy as jnp
from jax import lax
from jax.experimental import pallas as pl
from jax.experimental.pallas import tpu as pltpu
from jax.sharding import PartitionSpec as P

NSUB = 4
CAP = 4
MESH = pl.DeviceIdType.MESH


def device_tools(names):
    sizes = {name: lax.axis_size(name) for name in names}
    n_grp, n_gx, n_gy = sizes["grp"], sizes["gx"], sizes["gy"]
    grp, gx, gy = lax.axis_index("grp"), lax.axis_index("gx"), lax.axis_index("gy")
    bx = grp * n_gx + gx

    def at_row(row):
        return (row // n_gx, row % n_gx, gy)

    sides = (
        (bx > 0, at_row(jnp.maximum(bx - 1, 0))),
        (bx < n_grp * n_gx - 1, at_row(jnp.minimum(bx + 1, n_grp * n_gx - 1))),
        (gy > 0, (grp, gx, jnp.maximum(gy - 1, 0))),
        (gy < n_gy - 1, (grp, gx, jnp.minimum(gy + 1, n_gy - 1))),
    )
    return grp, gx, gy, n_grp, n_gx, n_gy, sides


def signal(semaphore, target):
    pl.semaphore_signal(semaphore, inc=1, device_id=target, device_id_type=MESH)


def enter(tools):
    grp, gx, gy, n_grp, n_gx, n_gy, sides = tools
    peers = n_gx * n_gy
    me = gx * n_gy + gy
    barrier = pltpu.get_barrier_semaphore()

    def greet(i, carry):
        peer = lax.rem(me + i, peers)
        signal(barrier, (grp, peer // n_gy, peer % n_gy))
        return carry

    lax.fori_loop(1, peers, greet, 0)
    for i in range(1, n_grp):
        signal(barrier, (lax.rem(grp + i, n_grp), gx, gy))
    cross_low = jnp.logical_and(gx == 0, grp > 0)
    cross_high = jnp.logical_and(gx == n_gx - 1, grp < n_grp - 1)

    @pl.when(cross_low)
    def _():
        signal(barrier, sides[0][1])

    @pl.when(cross_high)
    def _():
        signal(barrier, sides[1][1])

    extra = cross_low.astype(jnp.int32) + cross_high.astype(jnp.int32)
    pl.semaphore_wait(barrier, peers - 1 + n_grp - 1 + extra)


class Gather:
    def __init__(self, tools, source, rows, send_sems, recv_sems):
        self.tools, self.source, self.rows = tools, source, rows
        self.send_sems, self.recv_sems = send_sems, recv_sems
        self.peers = tools[4] * tools[5]
        self.me = tools[1] * tools[5] + tools[2]

    def copy(self, peer, slot):
        n_gy = self.tools[5]
        return pltpu.make_async_remote_copy(
            src_ref=self.source,
            dst_ref=self.rows.at[slot],
            send_sem=self.send_sems.at[peer],
            recv_sem=self.recv_sems.at[slot],
            device_id=(self.tools[0], peer // n_gy, peer % n_gy),
            device_id_type=MESH,
        )

    def start(self, block):
        self.source[...] = block
        self.rows[self.me] = block

        def step(i, carry):
            self.copy(lax.rem(self.me + i, self.peers), self.me).start()
            return carry

        lax.fori_loop(1, self.peers, step, 0)

    def wait(self):
        def step(i, carry):
            peer = lax.rem(self.me + i, self.peers)
            self.copy(peer, peer).wait_recv()
            return carry

        lax.fori_loop(1, self.peers, step, 0)

    def finish(self):
        def step(i, carry):
            peer = lax.rem(self.me + i, self.peers)
            self.copy(peer, peer).wait_send()
            return carry

        lax.fori_loop(1, self.peers, step, 0)


class Rim:
    def __init__(self, tools, source, landing, send_sems, recv_sems):
        self.sides = tools[6]
        self.source, self.landing = source, landing
        self.send_sems, self.recv_sems = send_sems, recv_sems

    def copy(self, side, slot):
        return pltpu.make_async_remote_copy(
            src_ref=self.source.at[side],
            dst_ref=self.landing.at[slot],
            send_sem=self.send_sems.at[side],
            recv_sem=self.recv_sems.at[slot],
            device_id=self.sides[side][1],
            device_id_type=MESH,
        )

    def start(self, side):
        @pl.when(self.sides[side][0])
        def _():
            self.copy(side, side ^ 1).start()

    def wait(self, side):
        @pl.when(self.sides[side][0])
        def _():
            self.copy(side, side).wait_recv()

        @pl.when(jnp.logical_not(self.sides[side][0]))
        def _():
            self.landing[side] = jnp.zeros_like(self.landing[side])

    def finish(self):
        for side in range(4):
            @pl.when(self.sides[side][0])
            def _():
                self.copy(side, side).wait_send()


def stack_rows(rows):
    width = rows[0].shape[1]
    place = lax.broadcasted_iota(jnp.int32, (8, width), 0)
    out = jnp.zeros((8, width), jnp.float32)
    for i, row in enumerate(rows):
        out = jnp.where(place == i, row, out)
    return out


def send_edges(rim, fields):
    last, right = fields[0].shape[0] - 1, fields[0].shape[1] - 1
    rim.source[0] = stack_rows([f[0:1] for f in fields])
    rim.start(0)
    rim.source[1] = stack_rows([f[last:] for f in fields])
    rim.start(1)
    turned = [f.T for f in fields]
    rim.source[2] = stack_rows([f[0:1] for f in turned])
    rim.start(2)
    rim.source[3] = stack_rows([f[right:] for f in turned])
    rim.start(3)


def rim_values(rim, count, shape):
    for side in range(4):
        rim.wait(side)
    row_count, col_count = shape
    line = lax.broadcasted_iota(jnp.int32, (col_count, row_count), 0)
    result = []
    for i in range(count):
        low, high = rim.landing[0, i : i + 1], rim.landing[1, i : i + 1]
        west, east = rim.landing[2, i : i + 1], rim.landing[3, i : i + 1]
        side = jnp.where(line == 0, west, jnp.where(line == col_count - 1, east, 0.0)).T
        result.append((low, high, side))
    return result


def around(field, rim):
    low, high, side = rim
    row_count, col_count = field.shape
    row = lax.broadcasted_iota(jnp.int32, field.shape, 0)
    col = lax.broadcasted_iota(jnp.int32, field.shape, 1)
    return (
        jnp.where(row == row_count - 1, high, pltpu.roll(field, row_count - 1, 0)),
        jnp.where(row == 0, low, pltpu.roll(field, 1, 0)),
        jnp.where(col == col_count - 1, side, pltpu.roll(field, col_count - 1, 1)),
        jnp.where(col == 0, side, pltpu.roll(field, 1, 1)),
    )


def dot(a, b, a_dim, b_dim):
    return lax.dot_general(
        a, b, (((a_dim,), (b_dim,)), ((), ())),
        precision=lax.Precision.HIGHEST, preferred_element_type=jnp.float32,
    )


class Edge:
    def __init__(self, tools, first, sources, landings, send_sems, recv_sems):
        self.sides = tools[6][first : first + 2]
        self.sources, self.landings = sources, landings
        self.send_sems, self.recv_sems = send_sems, recv_sems

    def copy(self, side, slot):
        return pltpu.make_async_remote_copy(
            src_ref=self.sources[side],
            dst_ref=self.landings[slot],
            send_sem=self.send_sems.at[side],
            recv_sem=self.recv_sems.at[slot],
            device_id=self.sides[side][1],
            device_id_type=MESH,
        )

    def start(self):
        for side in range(2):
            @pl.when(self.sides[side][0])
            def _():
                self.copy(side, 1 - side).start()

    def wait(self):
        for side in range(2):
            @pl.when(self.sides[side][0])
            def _():
                self.copy(side, side).wait_recv()

            @pl.when(jnp.logical_not(self.sides[side][0]))
            def _():
                self.landings[side][...] = jnp.zeros(self.landings[side].shape, jnp.float32)

    def finish(self):
        for side in range(2):
            @pl.when(self.sides[side][0])
            def _():
                self.copy(side, side).wait_send()


def row_tiles(layers):
    half = len(layers) // 2
    count = layers[0].shape[0]
    row = lax.broadcasted_iota(jnp.int32, layers[0].shape, 0)
    low, high = [], []
    for a, b in zip(layers[:half], layers[half:]):
        turned = pltpu.roll(b, count // 2, 0)
        low.append(jnp.where(row < count // 2, a, turned))
        high.append(jnp.where(row < count // 2, turned, a))
    return low, high


def halo_tiles(from_low, from_high):
    count = from_low[0].shape[0]
    row = lax.broadcasted_iota(jnp.int32, from_low[0].shape, 0)
    first, second = [], []
    for low, high in zip(from_low, from_high):
        first.append(jnp.where(row < count // 2, high, low))
        second.append(pltpu.roll(jnp.where(row < count // 2, low, high), count // 2, 0))
    return first + second


def packed(layers):
    lane = lax.broadcasted_iota(jnp.int32, layers[0].shape, 1)
    out = jnp.zeros(layers[0].shape, jnp.float32)
    for g, layer in enumerate(layers):
        moved = pltpu.roll(layer, (2 * NSUB * g + NSUB) % layer.shape[1], 1)
        out = jnp.where(lane // (2 * NSUB) == g, moved, out)
    return out


def joined(left, right):
    lane = lax.broadcasted_iota(jnp.int32, left.shape, 1)
    return jnp.where(lane % (2 * NSUB) < NSUB, left, right)


def repeated(pack, slot):
    group = 2 * NSUB
    width = pack.shape[1]
    lane = lax.broadcasted_iota(jnp.int32, pack.shape, 1)
    out = jnp.where(lane // group == slot, pack, 0.0)
    reach = group
    while reach < width:
        out = out + pltpu.roll(out, reach, 1)
        reach *= 2
    return out


def row_ring(pair):
    main, halo = pair
    count = main.shape[0]
    row = lax.broadcasted_iota(jnp.int32, main.shape, 0)
    main_up, halo_up = pltpu.roll(main, count - 1, 0), pltpu.roll(halo, count - 1, 0)
    main_down, halo_down = pltpu.roll(main, 1, 0), pltpu.roll(halo, 1, 0)
    end, begin = row == count - 1, row == 0
    return (
        (jnp.where(end, halo_up, main_up), jnp.where(end, main_up, halo_up)),
        (jnp.where(begin, halo_down, main_down), jnp.where(begin, main_down, halo_down)),
    )


def ring_sides(pair, west=None, east=None):
    width = pair[0].shape[1]
    lane = lax.broadcasted_iota(jnp.int32, pair[0].shape, 1)
    up, down = row_ring(pair)
    right = [pltpu.roll(x, width - 1, 1) for x in pair]
    left = [pltpu.roll(x, 1, 1) for x in pair]
    if west is not None:
        right = [jnp.where(lane == width - 1, e, x) for e, x in zip(east, right)]
        left = [jnp.where(lane == 0, w, x) for w, x in zip(west, left)]
    return up, down, right, left


def ring_weights(mix, wet, mix_ends=(None, None), wet_ends=(None, None)):
    weights = []
    for mix_side, wet_side in zip(ring_sides(mix, *mix_ends), ring_sides(wet, *wet_ends)):
        weights.append([0.5 * (mix[t] + mix_side[t]) * wet[t] * wet_side[t] for t in range(2)])
    stay = [1.0 - (weights[0][t] + weights[1][t] + weights[2][t] + weights[3][t]) for t in range(2)]
    return weights, stay


def spread(pair, weights, west=None, east=None, tiles=2):
    sides, stay = ring_sides(pair, west, east), weights[1]
    out = []
    for t in range(tiles):
        total = stay[t] * pair[t]
        for weight, side in zip(weights[0], sides):
            total = total + weight[t] * side[t]
        out.append(total)
    return out


def column(pair, lane):
    return [x[:, lane : lane + 1] for x in pair]


def surface(fields, moved, cover, draft, tile):
    temp, salt, east, north = [f[tile] for f in fields]
    speed = jnp.sqrt(east * east + north * north + 0.01)
    freezing = -0.5 * salt + 0.3 * draft[tile] - 0.2
    melt = 0.5 * cover[tile] * (temp - freezing) * speed
    drag = 0.05 * cover[tile] * speed
    moved[0][tile] = moved[0][tile] - 0.3 * melt
    moved[1][tile] = moved[1][tile] - 0.2 * melt
    moved[2][tile] = moved[2][tile] - drag * east
    moved[3][tile] = moved[3][tile] - drag * north
    return melt


def slot_table(rows, me, peers, width):
    lane = lax.broadcasted_iota(jnp.int32, (1, width), 1)
    out = jnp.zeros((1, width), jnp.float32)
    for p in range(peers):
        turn = lax.rem(CAP * (p - me) + width, width)
        out = jnp.where(lane // CAP == p, pltpu.roll(rows[p], turn, 1), out)
    return out


def tall(row):
    return jnp.broadcast_to(row, (8, row.shape[1]))


class Ocean:
    def __init__(self, tools, state_ref, next_ref, halo_ref, weight_ref, buffers):
        self.tools, self.state, self.next = tools, state_ref, next_ref
        self.halo, self.weight_ref = halo_ref, weight_ref
        (row_src, row_land, col_src, col_land, row_send, row_recv, col_send, col_recv) = buffers
        self.row_src, self.row_land = row_src, row_land
        self.col_src, self.col_land = col_src, col_land
        self.group = state_ref.shape[2] // (2 * NSUB)
        self.packs = state_ref.shape[0] // self.group
        self.chunks = max(c for c in range(1, 4) if self.packs % c == 0)
        self.each = self.packs // self.chunks
        half = self.group // 2
        self.row_edges, self.col_edges = [], []
        for c in range(self.chunks):
            rows, cols = pl.ds(c * self.each * half, self.each * half), pl.ds(c * self.each, self.each)
            self.row_edges.append(Edge(
                tools, 0, [row_src.at[s, rows] for s in range(2)],
                [row_land.at[s, rows] for s in range(2)], row_send.at[c], row_recv.at[c],
            ))
            self.col_edges.append(Edge(
                tools, 2, [col_src.at[cols]] * 2,
                [col_land.at[s, cols] for s in range(2)], col_send.at[c], col_recv.at[c],
            ))

    def loop(self, c, step):
        def body(v, carry):
            step(v)
            return carry

        lax.fori_loop(c * self.each, (c + 1) * self.each, body, 0)

    def send_rows(self, c):
        half = self.group // 2

        def step(v):
            layers = [self.state[v * self.group + j] for j in range(self.group)]
            low, high = row_tiles(layers)
            for j in range(half):
                self.row_src[0, v * half + j] = low[j]
                self.row_src[1, v * half + j] = high[j]

        self.loop(c, step)
        self.row_edges[c].start()

    def send_columns(self, c):
        half = self.group // 2
        self.row_edges[c].wait()

        def step(v):
            low = [self.row_land[0, v * half + j] for j in range(half)]
            high = [self.row_land[1, v * half + j] for j in range(half)]
            halo = halo_tiles(low, high)
            for j in range(self.group):
                self.halo[v * self.group + j] = halo[j]
            self.col_src[v, 0] = packed([self.state[v * self.group + j] for j in range(self.group)])
            self.col_src[v, 1] = packed(halo)

        self.loop(c, step)
        self.col_edges[c].start()

    def compute(self, c):
        self.col_edges[c].wait()

        def weights_of(block):
            pick = [[self.weight_ref[block, k, t] for t in range(2)] for k in range(5)]
            return pick[:4], pick[4]

        def step(v):
            wings = []
            for block in (0, 2):
                pair = []
                for t in range(2):
                    own = self.col_src[v, t]
                    if block == 0:
                        pair.append(joined(self.col_land[0, v, t], own))
                    else:
                        pair.append(joined(own, self.col_land[1, v, t]))
                stages = [pair]
                weights = weights_of(block)
                for _ in range(NSUB - 1):
                    stages.append(spread(stages[-1], weights))
                wings.append(stages)
            weights = weights_of(1)
            for j in range(self.group):
                place = 2 * NSUB * j
                pair = [self.state[v * self.group + j], self.halo[v * self.group + j]]
                for s in range(NSUB):
                    west = column(wings[0][s], place + NSUB - 1)
                    east = column(wings[1][s], place + NSUB)
                    pair = spread(pair, weights, west, east, 1 if s == NSUB - 1 else 2)
                self.next[v * self.group + j] = pair[0]

        self.loop(c, step)

    def finish(self):
        for edge in self.row_edges + self.col_edges:
            edge.finish()


def top_exchange(tools, layers, src, land, send, recv):
    half = len(layers) // 2
    low, high = row_tiles(layers)
    for j in range(half):
        src[0, j] = low[j]
        src[1, j] = high[j]
    rows = Edge(tools, 0, [src.at[0], src.at[1]], [land.at[0], land.at[1]], send.at[0], recv.at[0])
    rows.start()
    rows.wait()
    halo = halo_tiles([land[0, j] for j in range(half)], [land[1, j] for j in range(half)])
    own = [packed(layers), packed(halo)]
    src[2, 0], src[2, 1] = own
    cols = Edge(
        tools, 2, [src.at[2, pl.ds(0, 2)]] * 2, [land.at[2, pl.ds(0, 2)], land.at[3, pl.ds(0, 2)]],
        send.at[1], recv.at[1],
    )
    cols.start()
    cols.wait()
    west = [joined(land[2, t], own[t]) for t in range(2)]
    east = [joined(own[t], land[3, t]) for t in range(2)]
    blocks = [[[repeated(x, i) for x in west] for i in range(len(layers))]]
    blocks.append([[layers[i], halo[i]] for i in range(len(layers))])
    blocks.append([[repeated(x, i) for x in east] for i in range(len(layers))])
    return blocks, (rows, cols)


def top_steps(blocks, weight_ref, levels, next_ref):
    def ends(i):
        return column(blocks[0][i], NSUB - 1), column(blocks[2][i], NSUB)

    weights = [
        ring_weights(blocks[0][4], blocks[0][5]),
        ring_weights(blocks[1][4], blocks[1][5], ends(4), ends(5)),
        ring_weights(blocks[2][4], blocks[2][5]),
    ]
    for b in range(3):
        for t in range(2):
            for k in range(4):
                weight_ref[b, k, t] = weights[b][0][k][t]
            weight_ref[b, 4, t] = weights[b][1][t]
    fields = [block[:4] for block in blocks]
    total = 0.0
    for s in range(NSUB):
        moved = [[], [], []]
        for i in range(4):
            moved[0].append(spread(fields[0][i], weights[0]))
            west, east = column(fields[0][i], NSUB - 1), column(fields[2][i], NSUB)
            moved[1].append(spread(fields[1][i], weights[1], west, east))
            moved[2].append(spread(fields[2][i], weights[2]))
        for b in range(3):
            for t in range(2):
                melt = surface(fields[b], moved[b], blocks[b][6], blocks[b][7], t)
                if b == 1 and t == 0:
                    total = total + melt
        fields = moved
    return [fields[1][i][0] for i in range(4)], total / NSUB


def step_kernel(
    levels,
    state_ref,
    mix_ref,
    wet_ref,
    cell_ref,
    slot_ref,
    node_ref,
    thick_ref,
    visc_ref,
    fric_ref,
    ground_ref,
    coup_ref,
    drive_ref,
    guess_ref,
    next_ref,
    mean_ref,
    vel_ref,
    res_ref,
    halo_ref,
    weight_ref,
    row_src,
    row_land,
    col_src,
    col_land,
    top_src,
    top_land,
    list_src,
    list_rows,
    sum_src,
    sum_rows,
    half_src,
    half_rows,
    edge_src,
    edge_land,
    row_send,
    row_recv,
    col_send,
    col_recv,
    top_send,
    top_recv,
    list_send,
    list_recv,
    sum_send,
    sum_recv,
    half_send,
    half_recv,
    edge_send,
    edge_recv,
):
    tools = device_tools(("grp", "gx", "gy"))
    grp, gx, gy, n_grp, n_gx, n_gy, sides = tools
    enter(tools)
    me = gx * n_gy + gy
    peers = n_gx * n_gy
    shape = thick_ref.shape
    width = node_ref.shape[1]
    items = cell_ref.shape[1]
    node, cell = node_ref[...], cell_ref[...]
    gathers = [
        Gather(tools, list_src.at[e], list_rows.at[e], list_send.at[e], list_recv.at[e])
        for e in range(2)
    ]
    row_of = (
        lax.broadcasted_iota(jnp.int32, (shape[0], width), 0)
        == jnp.where(node < 0, -1, node // shape[1])
    ).astype(jnp.float32)
    col_of = (lax.broadcasted_iota(jnp.int32, (shape[1], width), 0) == node % shape[1]).astype(jnp.float32)
    at_node = dot(thick_ref[...].T, row_of, 1, 0)
    gathers[0].start(0.9 * jnp.sum(at_node * col_of, axis=0, keepdims=True))
    ocean = Ocean(
        tools, state_ref, next_ref, halo_ref, weight_ref,
        (row_src, row_land, col_src, col_land, row_send, row_recv, col_send, col_recv),
    )
    ocean.send_rows(0)
    row_count, col_count = mean_ref.shape
    item_row = (
        lax.broadcasted_iota(jnp.int32, (row_count, items), 0)
        == jnp.where(cell < 0, -1, cell // col_count)
    ).astype(jnp.float32)
    item_col = (lax.broadcasted_iota(jnp.int32, (col_count, items), 0) == cell % col_count).astype(jnp.float32)
    item_slot = (lax.broadcasted_iota(jnp.int32, (width, items), 0) == slot_ref[...]).astype(jnp.float32)
    cover = dot(item_row, item_col, 1, 1)
    gathers[0].wait()
    draft_item = dot(tall(slot_table(list_rows.at[0], me, peers, width)), item_slot, 1, 0)[0:1]
    draft_field = dot(item_row * draft_item, item_col, 1, 1)
    layers = [state_ref[i * levels] for i in range(4)]
    layers += [mix_ref[...], wet_ref[...].astype(jnp.float32), cover, draft_field]
    blocks, top_edges = top_exchange(tools, layers, top_src, top_land, top_send, top_recv)
    top_next, melt_mean = top_steps(blocks, weight_ref, levels, next_ref)
    mean_ref[...] = melt_mean
    melt_item = jnp.sum(dot(melt_mean, item_col, 1, 0) * item_row, axis=0, keepdims=True)
    gathers[1].start(dot(tall(melt_item), item_slot, 1, 1)[0:1])
    for c in range(1, ocean.chunks):
        ocean.send_rows(c)
    friction = fric_ref[...] * ground_ref[...].astype(jnp.float32) + 0.2
    cross = 0.9 * friction * coup_ref[...]
    ocean.send_columns(0)
    gathers[1].wait()
    melt = slot_table(list_rows.at[1], me, peers, width)
    melt_node = dot(row_of * melt, col_of, 1, 1)
    thinned = thick_ref[...] * jnp.exp(-0.3 * melt_node)
    depth_visc = visc_ref[...] * thinned
    guess = [guess_ref[0], guess_ref[1]]
    rims = [Rim(tools, edge_src.at[e], edge_land.at[e], edge_send.at[e], edge_recv.at[e]) for e in range(3)]
    send_edges(rims[0], [depth_visc] + guess)
    ocean.compute(0)
    values = rim_values(rims[0], 3, shape)
    weights = [0.5 * (depth_visc + beside) for beside in around(depth_visc, values[0])]
    diagonal = weights[0] + weights[1] + weights[2] + weights[3] + friction
    scale = 1.0 / diagonal

    def apply(vector, rim):
        out = []
        for i in range(2):
            beside = 0.0
            for weight, side in zip(weights, around(vector[i], rim[i])):
                beside = beside + weight * side
            out.append(diagonal * vector[i] - beside + cross * vector[1 - i])
        return out

    def half_sums(index, products):
        rows = [jnp.sum(a[0] * b[0] + a[1] * b[1], axis=0, keepdims=True) for a, b in products]
        part = Gather(tools, sum_src.at[index], sum_rows.at[index], sum_send.at[index], sum_recv.at[index])
        part.start(stack_rows(rows))
        return part

    def whole_sums(index, part, count):
        part.wait()
        total = jnp.sum(sum_rows[index], axis=0)
        half_src[index] = total
        copies = []
        for i in range(1, n_grp):
            copies.append(pltpu.make_async_remote_copy(
                src_ref=half_src.at[index], dst_ref=half_rows.at[index, i - 1],
                send_sem=half_send.at[index, i - 1], recv_sem=half_recv.at[index, i - 1],
                device_id=(lax.rem(grp + i, n_grp), gx, gy), device_id_type=MESH,
            ))
            copies[-1].start()
        for i, copy in enumerate(copies):
            copy.wait()
            total = total + half_rows[index, i]
        summed = jnp.sum(total, axis=1, keepdims=True)
        return [summed[i : i + 1] for i in range(count)]

    image = apply(guess, values[1:])
    residual = [drive_ref[i] * thinned - image[i] for i in range(2)]
    precond = [residual[i] * scale for i in range(2)]
    send_edges(rims[1], precond)
    if ocean.chunks > 1:
        ocean.send_columns(1)
    edge_z = rim_values(rims[1], 2, shape)
    image = apply(precond, edge_z)
    scaled = [image[i] * scale for i in range(2)]
    part = half_sums(0, [(residual, precond), (precond, image)])
    send_edges(rims[2], scaled)
    edge_y = rim_values(rims[2], 2, shape)
    if ocean.chunks > 1:
        ocean.compute(1)
    norm, curve = whole_sums(0, part, 2)
    step = norm / curve
    velocity = [guess[i] + step * precond[i] for i in range(2)]
    residual = [residual[i] - step * image[i] for i in range(2)]
    next_precond = [residual[i] * scale for i in range(2)]
    edge = [tuple(z - step * y for z, y in zip(edge_z[i], edge_y[i])) for i in range(2)]
    next_image = apply(next_precond, edge)
    second = half_sums(1, [(residual, next_precond), (next_precond, next_image), (next_precond, image)])
    for c in range(2, ocean.chunks):
        ocean.send_columns(c)
    norm_next, own_curve, mixed = whole_sums(1, second, 3)
    ratio = norm_next / norm
    step = norm_next / (own_curve + 2.0 * ratio * mixed + ratio * ratio * curve)
    for i in range(2):
        vel_ref[i] = velocity[i] + step * (next_precond[i] + ratio * precond[i])
        res_ref[i] = residual[i] - step * (next_image[i] + ratio * image[i])
    for c in range(2, ocean.chunks):
        ocean.compute(c)
    for i in range(4):
        next_ref[i * levels] = top_next[i]
    ocean.finish()
    for edge in top_edges:
        edge.finish()
    for gather in gathers:
        gather.finish()
    part.finish()
    second.finish()
    for rim in rims:
        rim.finish()


def whole_step(arrays, levels):
    n_grp, n_gx, n_gy = lax.axis_size("grp"), lax.axis_size("gx"), lax.axis_size("gy")
    peers = n_gx * n_gy
    state, mix, guess = arrays[0], arrays[1], arrays[12]
    width, cols = arrays[5].shape[1], guess.shape[2]
    layer_total, row_count, col_count = state.shape
    group = col_count // (2 * NSUB)
    packs = layer_total // group
    vmem = pl.BlockSpec(memory_space=pltpu.VMEM)
    dma = pltpu.SemaphoreType.DMA
    f32 = jnp.float32

    def buffer(*dims):
        return pltpu.VMEM(dims, f32)

    tile = (row_count, col_count)
    return pl.pallas_call(
        functools.partial(step_kernel, levels),
        out_shape=[jax.ShapeDtypeStruct(a.shape, f32) for a in (state, mix, guess, guess)],
        in_specs=[vmem] * 13,
        out_specs=[vmem] * 4,
        scratch_shapes=[
            buffer(layer_total, *tile),
            buffer(3, 5, 2, *tile),
            buffer(2, layer_total // 2, *tile),
            buffer(2, layer_total // 2, *tile),
            buffer(packs, 2, *tile),
            buffer(2, packs, 2, *tile),
            buffer(3, 4, *tile),
            buffer(4, 4, *tile),
            buffer(2, 1, width),
            buffer(2, peers, 1, width),
            buffer(2, 8, cols),
            buffer(2, peers, 8, cols),
            buffer(2, 8, cols),
            buffer(2, n_grp - 1, 8, cols),
            buffer(3, 4, 8, cols),
            buffer(3, 4, 8, cols),
            dma((3, 2)),
            dma((3, 2)),
            dma((3, 2)),
            dma((3, 2)),
            dma((2, 2)),
            dma((2, 2)),
            dma((2, peers)),
            dma((2, peers)),
            dma((2, peers)),
            dma((2, peers)),
            dma((2, n_grp - 1)),
            dma((2, n_grp - 1)),
            dma((3, 4)),
            dma((3, 4)),
        ],
        compiler_params=pltpu.CompilerParams(
            collective_id=0, has_side_effects=True, vmem_limit_bytes=40 * 1024 * 1024
        ),
    )(*arrays)


def shards(
    ocean_state,
    diffusivity,
    wet_mask,
    coast_column,
    coast_slot,
    owner_node,
    thickness,
    viscosity,
    friction,
    grounded,
    coupling,
    driving,
    first_guess,
):
    field_count, level_count, row_count, col_count = ocean_state.shape

    def lane_row(values):
        flat = values.reshape(1, -1)
        return jnp.pad(flat, ((0, 0), (0, -flat.shape[1] % 128)), constant_values=-1)

    fields, melt_mean, velocity, residual = whole_step(
        (
            ocean_state.reshape(-1, row_count, col_count),
            diffusivity,
            wet_mask,
            lane_row(coast_column),
            lane_row(coast_slot),
            lane_row(owner_node),
            thickness,
            viscosity,
            friction,
            grounded,
            coupling,
            driving,
            first_guess,
        ),
        level_count,
    )
    return (fields.reshape(ocean_state.shape), melt_mean, velocity, residual)


def solution(mesh):
    in_specs = (
        P(None, None, ("grp", "gx"), "gy"),
        P(("grp", "gx"), "gy"),
        P(("grp", "gx"), "gy"),
        P(("grp", "gx"), "gy", None),
        P(("grp", "gx"), "gy", None),
        P(("grp", "gx"), "gy", None, None),
        P(("grp", "gx"), "gy"),
        P(("grp", "gx"), "gy"),
        P(("grp", "gx"), "gy"),
        P(("grp", "gx"), "gy"),
        P(("grp", "gx"), "gy"),
        P(None, ("grp", "gx"), "gy"),
        P(None, ("grp", "gx"), "gy"),
    )
    out_specs = (
        P(None, None, ("grp", "gx"), "gy"),
        P(("grp", "gx"), "gy"),
        P(None, ("grp", "gx"), "gy"),
        P(None, ("grp", "gx"), "gy"),
    )
    return jax.shard_map(shards, mesh=mesh, in_specs=in_specs, out_specs=out_specs, check_vma=False)
```

```python
import functools

import jax
import jax.numpy as jnp
from jax import lax
from jax.experimental import pallas as pl
from jax.experimental.pallas import tpu as pltpu
from jax.sharding import PartitionSpec as P

NSUB = 4
CAP = 4
BATCH = 8
MESH = pl.DeviceIdType.MESH


def device_tools(names):
    sizes = {name: lax.axis_size(name) for name in names}
    n_grp, n_gx, n_gy = sizes["grp"], sizes["gx"], sizes["gy"]
    grp, gx, gy = lax.axis_index("grp"), lax.axis_index("gx"), lax.axis_index("gy")
    bx = grp * n_gx + gx

    def at_row(row):
        return (row // n_gx, row % n_gx, gy)

    sides = (
        (bx > 0, at_row(jnp.maximum(bx - 1, 0))),
        (bx < n_grp * n_gx - 1, at_row(jnp.minimum(bx + 1, n_grp * n_gx - 1))),
        (gy > 0, (grp, gx, jnp.maximum(gy - 1, 0))),
        (gy < n_gy - 1, (grp, gx, jnp.minimum(gy + 1, n_gy - 1))),
    )
    return grp, gx, gy, n_grp, n_gx, n_gy, sides


def signal(semaphore, target):
    pl.semaphore_signal(semaphore, inc=1, device_id=target, device_id_type=MESH)


def enter(tools):
    grp, gx, gy, n_grp, n_gx, n_gy, sides = tools
    peers = n_gx * n_gy
    me = gx * n_gy + gy
    barrier = pltpu.get_barrier_semaphore()

    def greet(i, carry):
        peer = lax.rem(me + i, peers)
        signal(barrier, (grp, peer // n_gy, peer % n_gy))
        return carry

    lax.fori_loop(1, peers, greet, 0)
    for i in range(1, n_grp):
        signal(barrier, (lax.rem(grp + i, n_grp), gx, gy))
    cross_low = jnp.logical_and(gx == 0, grp > 0)
    cross_high = jnp.logical_and(gx == n_gx - 1, grp < n_grp - 1)

    @pl.when(cross_low)
    def _():
        signal(barrier, sides[0][1])

    @pl.when(cross_high)
    def _():
        signal(barrier, sides[1][1])

    extra = cross_low.astype(jnp.int32) + cross_high.astype(jnp.int32)
    pl.semaphore_wait(barrier, peers - 1 + n_grp - 1 + extra)


class Gather:
    def __init__(self, tools, source, rows, send_sems, recv_sems):
        self.tools, self.source, self.rows = tools, source, rows
        self.send_sems, self.recv_sems = send_sems, recv_sems
        self.peers = tools[4] * tools[5]
        self.me = tools[1] * tools[5] + tools[2]

    def copy(self, peer, slot):
        n_gy = self.tools[5]
        return pltpu.make_async_remote_copy(
            src_ref=self.source,
            dst_ref=self.rows.at[slot],
            send_sem=self.send_sems.at[peer],
            recv_sem=self.recv_sems.at[slot],
            device_id=(self.tools[0], peer // n_gy, peer % n_gy),
            device_id_type=MESH,
        )

    def start(self, block):
        self.source[...] = block
        self.rows[self.me] = block

        def step(i, carry):
            self.copy(lax.rem(self.me + i, self.peers), self.me).start()
            return carry

        lax.fori_loop(1, self.peers, step, 0)

    def wait(self):
        def step(i, carry):
            peer = lax.rem(self.me + i, self.peers)
            self.copy(peer, peer).wait_recv()
            return carry

        lax.fori_loop(1, self.peers, step, 0)

    def finish(self):
        def step(i, carry):
            peer = lax.rem(self.me + i, self.peers)
            self.copy(peer, peer).wait_send()
            return carry

        lax.fori_loop(1, self.peers, step, 0)


class Rim:
    def __init__(self, tools, source, landing, send_sems, recv_sems):
        self.sides = tools[6]
        self.source, self.landing = source, landing
        self.send_sems, self.recv_sems = send_sems, recv_sems

    def copy(self, side, slot):
        return pltpu.make_async_remote_copy(
            src_ref=self.source.at[side],
            dst_ref=self.landing.at[slot],
            send_sem=self.send_sems.at[side],
            recv_sem=self.recv_sems.at[slot],
            device_id=self.sides[side][1],
            device_id_type=MESH,
        )

    def start(self, side):
        @pl.when(self.sides[side][0])
        def _():
            self.copy(side, side ^ 1).start()

    def wait(self, side):
        @pl.when(self.sides[side][0])
        def _():
            self.copy(side, side).wait_recv()

        @pl.when(jnp.logical_not(self.sides[side][0]))
        def _():
            self.landing[side] = jnp.zeros_like(self.landing[side])

    def finish(self):
        for side in range(4):
            @pl.when(self.sides[side][0])
            def _():
                self.copy(side, side).wait_send()


def stack_rows(rows):
    width = rows[0].shape[1]
    place = lax.broadcasted_iota(jnp.int32, (8, width), 0)
    out = jnp.zeros((8, width), jnp.float32)
    for i, row in enumerate(rows):
        out = jnp.where(place == i, row, out)
    return out


def send_edges(rim, fields):
    last, right = fields[0].shape[0] - 1, fields[0].shape[1] - 1
    rim.source[0] = stack_rows([f[0:1] for f in fields])
    rim.start(0)
    rim.source[1] = stack_rows([f[last:] for f in fields])
    rim.start(1)
    turned = [f.T for f in fields]
    rim.source[2] = stack_rows([f[0:1] for f in turned])
    rim.start(2)
    rim.source[3] = stack_rows([f[right:] for f in turned])
    rim.start(3)


def rim_values(rim, count, shape):
    for side in range(4):
        rim.wait(side)
    row_count, col_count = shape
    line = lax.broadcasted_iota(jnp.int32, (col_count, row_count), 0)
    result = []
    for i in range(count):
        low, high = rim.landing[0, i : i + 1], rim.landing[1, i : i + 1]
        west, east = rim.landing[2, i : i + 1], rim.landing[3, i : i + 1]
        side = jnp.where(line == 0, west, jnp.where(line == col_count - 1, east, 0.0)).T
        result.append((low, high, side))
    return result


def around(field, rim):
    low, high, side = rim
    row_count, col_count = field.shape
    row = lax.broadcasted_iota(jnp.int32, field.shape, 0)
    col = lax.broadcasted_iota(jnp.int32, field.shape, 1)
    return (
        jnp.where(row == row_count - 1, high, pltpu.roll(field, row_count - 1, 0)),
        jnp.where(row == 0, low, pltpu.roll(field, 1, 0)),
        jnp.where(col == col_count - 1, side, pltpu.roll(field, col_count - 1, 1)),
        jnp.where(col == 0, side, pltpu.roll(field, 1, 1)),
    )


def dot(a, b, a_dim, b_dim):
    return lax.dot_general(
        a, b, (((a_dim,), (b_dim,)), ((), ())),
        precision=lax.Precision.HIGHEST, preferred_element_type=jnp.float32,
    )


class Edge:
    def __init__(self, tools, first, sources, landings, send_sems, recv_sems):
        self.sides = tools[6][first : first + 2]
        self.sources, self.landings = sources, landings
        self.send_sems, self.recv_sems = send_sems, recv_sems

    def copy(self, side, slot):
        return pltpu.make_async_remote_copy(
            src_ref=self.sources[side],
            dst_ref=self.landings[slot],
            send_sem=self.send_sems.at[side],
            recv_sem=self.recv_sems.at[slot],
            device_id=self.sides[side][1],
            device_id_type=MESH,
        )

    def start(self):
        for side in range(2):
            @pl.when(self.sides[side][0])
            def _():
                self.copy(side, 1 - side).start()

    def wait(self):
        for side in range(2):
            @pl.when(self.sides[side][0])
            def _():
                self.copy(side, side).wait_recv()

            @pl.when(jnp.logical_not(self.sides[side][0]))
            def _():
                self.landings[side][...] = jnp.zeros(self.landings[side].shape, jnp.float32)

    def finish(self):
        for side in range(2):
            @pl.when(self.sides[side][0])
            def _():
                self.copy(side, side).wait_send()


def row_tiles(layers):
    half = len(layers) // 2
    count = layers[0].shape[0]
    row = lax.broadcasted_iota(jnp.int32, layers[0].shape, 0)
    low, high = [], []
    for a, b in zip(layers[:half], layers[half:]):
        turned = pltpu.roll(b, count // 2, 0)
        low.append(jnp.where(row < count // 2, a, turned))
        high.append(jnp.where(row < count // 2, turned, a))
    return low, high


def halo_tiles(from_low, from_high):
    count = from_low[0].shape[0]
    row = lax.broadcasted_iota(jnp.int32, from_low[0].shape, 0)
    first, second = [], []
    for low, high in zip(from_low, from_high):
        first.append(jnp.where(row < count // 2, high, low))
        second.append(pltpu.roll(jnp.where(row < count // 2, low, high), count // 2, 0))
    return first + second


def packed(layers):
    lane = lax.broadcasted_iota(jnp.int32, layers[0].shape, 1)
    out = jnp.zeros(layers[0].shape, jnp.float32)
    for g, layer in enumerate(layers):
        moved = pltpu.roll(layer, (2 * NSUB * g + NSUB) % layer.shape[1], 1)
        out = jnp.where(lane // (2 * NSUB) == g, moved, out)
    return out


def joined(left, right):
    lane = lax.broadcasted_iota(jnp.int32, left.shape, 1)
    return jnp.where(lane % (2 * NSUB) < NSUB, left, right)


def repeated(pack, slot):
    group = 2 * NSUB
    width = pack.shape[1]
    lane = lax.broadcasted_iota(jnp.int32, pack.shape, 1)
    out = jnp.where(lane // group == slot, pack, 0.0)
    reach = group
    while reach < width:
        out = out + pltpu.roll(out, reach, 1)
        reach *= 2
    return out


def row_ring(pair):
    main, halo = pair
    count = main.shape[0]
    row = lax.broadcasted_iota(jnp.int32, main.shape, 0)
    main_up, halo_up = pltpu.roll(main, count - 1, 0), pltpu.roll(halo, count - 1, 0)
    main_down, halo_down = pltpu.roll(main, 1, 0), pltpu.roll(halo, 1, 0)
    end, begin = row == count - 1, row == 0
    return (
        (jnp.where(end, halo_up, main_up), jnp.where(end, main_up, halo_up)),
        (jnp.where(begin, halo_down, main_down), jnp.where(begin, main_down, halo_down)),
    )


def ring_sides(pair, west=None, east=None):
    width = pair[0].shape[1]
    lane = lax.broadcasted_iota(jnp.int32, pair[0].shape, 1)
    up, down = row_ring(pair)
    right = [pltpu.roll(x, width - 1, 1) for x in pair]
    left = [pltpu.roll(x, 1, 1) for x in pair]
    if west is not None:
        right = [jnp.where(lane == width - 1, e, x) for e, x in zip(east, right)]
        left = [jnp.where(lane == 0, w, x) for w, x in zip(west, left)]
    return up, down, right, left


def ring_weights(mix, wet, mix_ends=(None, None), wet_ends=(None, None)):
    weights = []
    for mix_side, wet_side in zip(ring_sides(mix, *mix_ends), ring_sides(wet, *wet_ends)):
        weights.append([0.5 * (mix[t] + mix_side[t]) * wet[t] * wet_side[t] for t in range(2)])
    stay = [1.0 - (weights[0][t] + weights[1][t] + weights[2][t] + weights[3][t]) for t in range(2)]
    return weights, stay


def spread(pair, weights, west=None, east=None, tiles=2):
    sides, stay = ring_sides(pair, west, east), weights[1]
    out = []
    for t in range(tiles):
        total = stay[t] * pair[t]
        for weight, side in zip(weights[0], sides):
            total = total + weight[t] * side[t]
        out.append(total)
    return out


def spread_rim(pair, weights, rim, tiles):
    width = pair[0].shape[1]
    lane = lax.broadcasted_iota(jnp.int32, pair[0].shape, 1)
    up, down = row_ring(pair)
    out = []
    for t in range(tiles):
        right = pltpu.roll(jnp.where(lane == 0, rim[t], pair[t]), width - 1, 1)
        left = pltpu.roll(jnp.where(lane == width - 1, rim[t], pair[t]), 1, 1)
        rows = weights[0][0][t] * up[t] + weights[0][1][t] * down[t]
        cols = weights[0][2][t] * right + weights[0][3][t] * left
        out.append(weights[1][t] * pair[t] + (rows + cols))
    return out


def column(pair, lane):
    return [x[:, lane : lane + 1] for x in pair]


def surface(fields, moved, cover, draft, tile):
    temp, salt, east, north = [f[tile] for f in fields]
    speed = jnp.sqrt(east * east + north * north + 0.01)
    freezing = -0.5 * salt + 0.3 * draft[tile] - 0.2
    melt = 0.5 * cover[tile] * (temp - freezing) * speed
    drag = 0.05 * cover[tile] * speed
    moved[0][tile] = moved[0][tile] - 0.3 * melt
    moved[1][tile] = moved[1][tile] - 0.2 * melt
    moved[2][tile] = moved[2][tile] - drag * east
    moved[3][tile] = moved[3][tile] - drag * north
    return melt


def slot_table(rows, me, peers, width):
    lane = lax.broadcasted_iota(jnp.int32, (1, width), 1)
    out = jnp.zeros((1, width), jnp.float32)
    for p in range(peers):
        turn = lax.rem(CAP * (p - me) + width, width)
        out = jnp.where(lane // CAP == p, pltpu.roll(rows[p], turn, 1), out)
    return out


def tall(row):
    return jnp.broadcast_to(row, (8, row.shape[1]))


class Ocean:
    def __init__(self, tools, state_ref, next_ref, halo_ref, weight_ref, buffers):
        self.tools, self.state, self.next = tools, state_ref, next_ref
        self.halo, self.weight_ref = halo_ref, weight_ref
        (row_src, row_land, col_src, col_land, row_send, row_recv, col_send, col_recv) = buffers
        self.row_src, self.row_land = row_src, row_land
        self.col_src, self.col_land = col_src, col_land
        self.group = state_ref.shape[2] // (2 * NSUB)
        self.packs = state_ref.shape[0] // self.group
        self.chunks = max(c for c in range(1, 4) if self.packs % c == 0)
        self.each = self.packs // self.chunks
        half = self.group // 2
        self.row_edges, self.col_edges = [], []
        for c in range(self.chunks):
            rows, cols = pl.ds(c * self.each * half, self.each * half), pl.ds(c * self.each, self.each)
            self.row_edges.append(Edge(
                tools, 0, [row_src.at[s, rows] for s in range(2)],
                [row_land.at[s, rows] for s in range(2)], row_send.at[c], row_recv.at[c],
            ))
            self.col_edges.append(Edge(
                tools, 2, [col_src.at[cols]] * 2,
                [col_land.at[s, cols] for s in range(2)], col_send.at[c], col_recv.at[c],
            ))

    def loop(self, c, step):
        def body(v, carry):
            step(v)
            return carry

        lax.fori_loop(c * self.each, (c + 1) * self.each, body, 0)

    def send_rows(self, c):
        half = self.group // 2

        def step(v):
            layers = [self.state[v * self.group + j] for j in range(self.group)]
            low, high = row_tiles(layers)
            for j in range(half):
                self.row_src[0, v * half + j] = low[j]
                self.row_src[1, v * half + j] = high[j]

        self.loop(c, step)
        self.row_edges[c].start()

    def send_columns(self, c):
        half = self.group // 2
        self.row_edges[c].wait()

        def step(v):
            low = [self.row_land[0, v * half + j] for j in range(half)]
            high = [self.row_land[1, v * half + j] for j in range(half)]
            halo = halo_tiles(low, high)
            for j in range(self.group):
                self.halo[v * self.group + j] = halo[j]
            self.col_src[v, 0] = packed([self.state[v * self.group + j] for j in range(self.group)])
            self.col_src[v, 1] = packed(halo)

        self.loop(c, step)
        self.col_edges[c].start()

    def compute(self, c):
        self.col_edges[c].wait()

        def weights_of(block):
            pick = [[self.weight_ref[block, k, t] for t in range(2)] for k in range(5)]
            return pick[:4], pick[4]

        def step(v):
            wings = []
            for block in (0, 2):
                pair = []
                for t in range(2):
                    own = self.col_src[v, t]
                    if block == 0:
                        pair.append(joined(self.col_land[0, v, t], own))
                    else:
                        pair.append(joined(own, self.col_land[1, v, t]))
                stages = [pair]
                weights = weights_of(block)
                for _ in range(NSUB - 1):
                    stages.append(spread(stages[-1], weights))
                wings.append(stages)
            weights = weights_of(1)
            ends = [
                [joined(wings[0][s][t], wings[1][s][t]) for t in range(2)] for s in range(NSUB)
            ]
            width = ends[0][0].shape[1]
            for first in range(0, self.group, BATCH):
                batch = range(first, min(first + BATCH, self.group))
                pairs = [
                    [self.state[v * self.group + j], self.halo[v * self.group + j]] for j in batch
                ]
                for s in range(NSUB):
                    tiles = 1 if s == NSUB - 1 else 2
                    moved = []
                    for j, pair in zip(batch, pairs):
                        turn = (2 * width - NSUB - 2 * NSUB * j) % width
                        rim = [pltpu.roll(ends[s][t], turn, 1) for t in range(tiles)]
                        moved.append(spread_rim(pair, weights, rim, tiles))
                    pairs = moved
                for j, pair in zip(batch, pairs):
                    self.next[v * self.group + j] = pair[0]

        self.loop(c, step)

    def finish(self):
        for edge in self.row_edges + self.col_edges:
            edge.finish()


def top_exchange(tools, layers, src, land, send, recv):
    half = len(layers) // 2
    low, high = row_tiles(layers)
    for j in range(half):
        src[0, j] = low[j]
        src[1, j] = high[j]
    rows = Edge(tools, 0, [src.at[0], src.at[1]], [land.at[0], land.at[1]], send.at[0], recv.at[0])
    rows.start()
    rows.wait()
    halo = halo_tiles([land[0, j] for j in range(half)], [land[1, j] for j in range(half)])
    own = [packed(layers), packed(halo)]
    src[2, 0], src[2, 1] = own
    cols = Edge(
        tools, 2, [src.at[2, pl.ds(0, 2)]] * 2, [land.at[2, pl.ds(0, 2)], land.at[3, pl.ds(0, 2)]],
        send.at[1], recv.at[1],
    )
    cols.start()
    cols.wait()
    west = [joined(land[2, t], own[t]) for t in range(2)]
    east = [joined(own[t], land[3, t]) for t in range(2)]
    blocks = [[[repeated(x, i) for x in west] for i in range(len(layers))]]
    blocks.append([[layers[i], halo[i]] for i in range(len(layers))])
    blocks.append([[repeated(x, i) for x in east] for i in range(len(layers))])
    return blocks, (rows, cols)


def top_steps(blocks, weight_ref, levels, next_ref):
    def ends(i):
        return column(blocks[0][i], NSUB - 1), column(blocks[2][i], NSUB)

    weights = [
        ring_weights(blocks[0][4], blocks[0][5]),
        ring_weights(blocks[1][4], blocks[1][5], ends(4), ends(5)),
        ring_weights(blocks[2][4], blocks[2][5]),
    ]
    for b in range(3):
        for t in range(2):
            for k in range(4):
                weight_ref[b, k, t] = weights[b][0][k][t]
            weight_ref[b, 4, t] = weights[b][1][t]
    fields = [block[:4] for block in blocks]
    total = 0.0
    for s in range(NSUB):
        moved = [[], [], []]
        for i in range(4):
            moved[0].append(spread(fields[0][i], weights[0]))
            west, east = column(fields[0][i], NSUB - 1), column(fields[2][i], NSUB)
            moved[1].append(spread(fields[1][i], weights[1], west, east))
            moved[2].append(spread(fields[2][i], weights[2]))
        for b in range(3):
            for t in range(2):
                melt = surface(fields[b], moved[b], blocks[b][6], blocks[b][7], t)
                if b == 1 and t == 0:
                    total = total + melt
        fields = moved
    return [fields[1][i][0] for i in range(4)], total / NSUB


def step_kernel(
    levels,
    state_hbm,
    mix_ref,
    wet_ref,
    cell_ref,
    slot_ref,
    node_ref,
    thick_hbm,
    visc_hbm,
    fric_hbm,
    ground_hbm,
    coup_hbm,
    drive_hbm,
    guess_hbm,
    next_ref,
    mean_ref,
    vel_ref,
    res_ref,
    state_ref,
    thick_ref,
    visc_ref,
    fric_ref,
    ground_ref,
    coup_ref,
    drive_ref,
    guess_ref,
    load_sems,
    halo_ref,
    weight_ref,
    row_src,
    row_land,
    col_src,
    col_land,
    top_src,
    top_land,
    list_src,
    list_rows,
    sum_src,
    sum_rows,
    half_src,
    half_rows,
    edge_src,
    edge_land,
    row_send,
    row_recv,
    col_send,
    col_recv,
    top_send,
    top_recv,
    list_send,
    list_recv,
    sum_send,
    sum_recv,
    half_send,
    half_recv,
    edge_send,
    edge_recv,
):
    tools = device_tools(("grp", "gx", "gy"))
    grp, gx, gy, n_grp, n_gx, n_gy, sides = tools
    pairs = (
        (thick_hbm, thick_ref),
        (state_hbm, state_ref),
        (visc_hbm, visc_ref),
        (guess_hbm, guess_ref),
        (drive_hbm, drive_ref),
        (fric_hbm, fric_ref),
        (ground_hbm, ground_ref),
        (coup_hbm, coup_ref),
    )
    loads = [pltpu.make_async_copy(a, b, load_sems.at[i]) for i, (a, b) in enumerate(pairs)]
    for load in loads:
        load.start()
    enter(tools)
    me = gx * n_gy + gy
    peers = n_gx * n_gy
    shape = thick_ref.shape
    width = node_ref.shape[1]
    items = cell_ref.shape[1]
    node, cell = node_ref[...], cell_ref[...]
    gathers = [
        Gather(tools, list_src.at[e], list_rows.at[e], list_send.at[e], list_recv.at[e])
        for e in range(2)
    ]
    row_of = (
        lax.broadcasted_iota(jnp.int32, (shape[0], width), 0)
        == jnp.where(node < 0, -1, node // shape[1])
    ).astype(jnp.float32)
    col_of = (lax.broadcasted_iota(jnp.int32, (shape[1], width), 0) == node % shape[1]).astype(jnp.float32)
    loads[0].wait()
    at_node = dot(thick_ref[...].T, row_of, 1, 0)
    gathers[0].start(0.9 * jnp.sum(at_node * col_of, axis=0, keepdims=True))
    ocean = Ocean(
        tools, state_ref, next_ref, halo_ref, weight_ref,
        (row_src, row_land, col_src, col_land, row_send, row_recv, col_send, col_recv),
    )
    loads[1].wait()
    ocean.send_rows(0)
    row_count, col_count = mean_ref.shape
    item_row = (
        lax.broadcasted_iota(jnp.int32, (row_count, items), 0)
        == jnp.where(cell < 0, -1, cell // col_count)
    ).astype(jnp.float32)
    item_col = (lax.broadcasted_iota(jnp.int32, (col_count, items), 0) == cell % col_count).astype(jnp.float32)
    item_slot = (lax.broadcasted_iota(jnp.int32, (width, items), 0) == slot_ref[...]).astype(jnp.float32)
    cover = dot(item_row, item_col, 1, 1)
    gathers[0].wait()
    draft_item = dot(tall(slot_table(list_rows.at[0], me, peers, width)), item_slot, 1, 0)[0:1]
    draft_field = dot(item_row * draft_item, item_col, 1, 1)
    layers = [state_ref[i * levels] for i in range(4)]
    layers += [mix_ref[...], wet_ref[...].astype(jnp.float32), cover, draft_field]
    blocks, top_edges = top_exchange(tools, layers, top_src, top_land, top_send, top_recv)
    top_next, melt_mean = top_steps(blocks, weight_ref, levels, next_ref)
    mean_ref[...] = melt_mean
    melt_item = jnp.sum(dot(melt_mean, item_col, 1, 0) * item_row, axis=0, keepdims=True)
    gathers[1].start(dot(tall(melt_item), item_slot, 1, 1)[0:1])
    for c in range(1, ocean.chunks):
        ocean.send_rows(c)
    for load in loads[2:]:
        load.wait()
    friction = fric_ref[...] * ground_ref[...].astype(jnp.float32) + 0.2
    cross = 0.9 * friction * coup_ref[...]
    ocean.send_columns(0)
    gathers[1].wait()
    melt = slot_table(list_rows.at[1], me, peers, width)
    melt_node = dot(row_of * melt, col_of, 1, 1)
    thinned = thick_ref[...] * jnp.exp(-0.3 * melt_node)
    depth_visc = visc_ref[...] * thinned
    guess = [guess_ref[0], guess_ref[1]]
    rims = [Rim(tools, edge_src.at[e], edge_land.at[e], edge_send.at[e], edge_recv.at[e]) for e in range(3)]
    send_edges(rims[0], [depth_visc] + guess)
    ocean.compute(0)
    values = rim_values(rims[0], 3, shape)
    weights = [0.5 * (depth_visc + beside) for beside in around(depth_visc, values[0])]
    diagonal = weights[0] + weights[1] + weights[2] + weights[3] + friction
    scale = 1.0 / diagonal

    def apply(vector, rim):
        out = []
        for i in range(2):
            beside = 0.0
            for weight, side in zip(weights, around(vector[i], rim[i])):
                beside = beside + weight * side
            out.append(diagonal * vector[i] - beside + cross * vector[1 - i])
        return out

    def half_sums(index, products):
        rows = [jnp.sum(a[0] * b[0] + a[1] * b[1], axis=0, keepdims=True) for a, b in products]
        part = Gather(tools, sum_src.at[index], sum_rows.at[index], sum_send.at[index], sum_recv.at[index])
        part.start(stack_rows(rows))
        return part

    def whole_sums(index, part, count):
        part.wait()
        total = jnp.sum(sum_rows[index], axis=0)
        half_src[index] = total
        copies = []
        for i in range(1, n_grp):
            copies.append(pltpu.make_async_remote_copy(
                src_ref=half_src.at[index], dst_ref=half_rows.at[index, i - 1],
                send_sem=half_send.at[index, i - 1], recv_sem=half_recv.at[index, i - 1],
                device_id=(lax.rem(grp + i, n_grp), gx, gy), device_id_type=MESH,
            ))
            copies[-1].start()
        for i, copy in enumerate(copies):
            copy.wait()
            total = total + half_rows[index, i]
        summed = jnp.sum(total, axis=1, keepdims=True)
        return [summed[i : i + 1] for i in range(count)]

    image = apply(guess, values[1:])
    residual = [drive_ref[i] * thinned - image[i] for i in range(2)]
    precond = [residual[i] * scale for i in range(2)]
    send_edges(rims[1], precond)
    if ocean.chunks > 1:
        ocean.send_columns(1)
    edge_z = rim_values(rims[1], 2, shape)
    image = apply(precond, edge_z)
    scaled = [image[i] * scale for i in range(2)]
    part = half_sums(0, [(residual, precond), (precond, image)])
    send_edges(rims[2], scaled)
    edge_y = rim_values(rims[2], 2, shape)
    if ocean.chunks > 1:
        ocean.compute(1)
    norm, curve = whole_sums(0, part, 2)
    step = norm / curve
    velocity = [guess[i] + step * precond[i] for i in range(2)]
    residual = [residual[i] - step * image[i] for i in range(2)]
    next_precond = [residual[i] * scale for i in range(2)]
    edge = [tuple(z - step * y for z, y in zip(edge_z[i], edge_y[i])) for i in range(2)]
    next_image = apply(next_precond, edge)
    second = half_sums(1, [(residual, next_precond), (next_precond, next_image), (next_precond, image)])
    for c in range(2, ocean.chunks):
        ocean.send_columns(c)
    norm_next, own_curve, mixed = whole_sums(1, second, 3)
    ratio = norm_next / norm
    step = norm_next / (own_curve + 2.0 * ratio * mixed + ratio * ratio * curve)
    for i in range(2):
        vel_ref[i] = velocity[i] + step * (next_precond[i] + ratio * precond[i])
        res_ref[i] = residual[i] - step * (next_image[i] + ratio * image[i])
    for c in range(2, ocean.chunks):
        ocean.compute(c)
    for i in range(4):
        next_ref[i * levels] = top_next[i]
    ocean.finish()
    for edge in top_edges:
        edge.finish()
    for gather in gathers:
        gather.finish()
    part.finish()
    second.finish()
    for rim in rims:
        rim.finish()


def whole_step(arrays, levels):
    n_grp, n_gx, n_gy = lax.axis_size("grp"), lax.axis_size("gx"), lax.axis_size("gy")
    peers = n_gx * n_gy
    state, mix, guess = arrays[0], arrays[1], arrays[12]
    width, cols = arrays[5].shape[1], guess.shape[2]
    layer_total, row_count, col_count = state.shape
    group = col_count // (2 * NSUB)
    packs = layer_total // group
    vmem = pl.BlockSpec(memory_space=pltpu.VMEM)
    hbm = pl.BlockSpec(memory_space=pltpu.HBM)
    dma = pltpu.SemaphoreType.DMA
    f32 = jnp.float32

    def buffer(*dims):
        return pltpu.VMEM(dims, f32)

    tile = (row_count, col_count)
    return pl.pallas_call(
        functools.partial(step_kernel, levels),
        out_shape=[jax.ShapeDtypeStruct(a.shape, f32) for a in (state, mix, guess, guess)],
        in_specs=[hbm, vmem, vmem, vmem, vmem, vmem] + [hbm] * 7,
        out_specs=[vmem] * 4,
        scratch_shapes=[
            *(pltpu.VMEM(arrays[i].shape, arrays[i].dtype) for i in (0, 6, 7, 8, 9, 10, 11, 12)),
            dma((8,)),
            buffer(layer_total, *tile),
            buffer(3, 5, 2, *tile),
            buffer(2, layer_total // 2, *tile),
            buffer(2, layer_total // 2, *tile),
            buffer(packs, 2, *tile),
            buffer(2, packs, 2, *tile),
            buffer(3, 4, *tile),
            buffer(4, 4, *tile),
            buffer(2, 1, width),
            buffer(2, peers, 1, width),
            buffer(2, 8, cols),
            buffer(2, peers, 8, cols),
            buffer(2, 8, cols),
            buffer(2, n_grp - 1, 8, cols),
            buffer(3, 4, 8, cols),
            buffer(3, 4, 8, cols),
            dma((3, 2)),
            dma((3, 2)),
            dma((3, 2)),
            dma((3, 2)),
            dma((2, 2)),
            dma((2, 2)),
            dma((2, peers)),
            dma((2, peers)),
            dma((2, peers)),
            dma((2, peers)),
            dma((2, n_grp - 1)),
            dma((2, n_grp - 1)),
            dma((3, 4)),
            dma((3, 4)),
        ],
        compiler_params=pltpu.CompilerParams(
            collective_id=0, has_side_effects=True, vmem_limit_bytes=56 * 1024 * 1024
        ),
    )(*arrays)


def shards(
    ocean_state,
    diffusivity,
    wet_mask,
    coast_column,
    coast_slot,
    owner_node,
    thickness,
    viscosity,
    friction,
    grounded,
    coupling,
    driving,
    first_guess,
):
    field_count, level_count, row_count, col_count = ocean_state.shape

    def lane_row(values):
        flat = values.reshape(1, -1)
        return jnp.pad(flat, ((0, 0), (0, -flat.shape[1] % 128)), constant_values=-1)

    fields, melt_mean, velocity, residual = whole_step(
        (
            ocean_state.reshape(-1, row_count, col_count),
            diffusivity,
            wet_mask,
            lane_row(coast_column),
            lane_row(coast_slot),
            lane_row(owner_node),
            thickness,
            viscosity,
            friction,
            grounded,
            coupling,
            driving,
            first_guess,
        ),
        level_count,
    )
    return (fields.reshape(ocean_state.shape), melt_mean, velocity, residual)


def solution(mesh):
    in_specs = (
        P(None, None, ("grp", "gx"), "gy"),
        P(("grp", "gx"), "gy"),
        P(("grp", "gx"), "gy"),
        P(("grp", "gx"), "gy", None),
        P(("grp", "gx"), "gy", None),
        P(("grp", "gx"), "gy", None, None),
        P(("grp", "gx"), "gy"),
        P(("grp", "gx"), "gy"),
        P(("grp", "gx"), "gy"),
        P(("grp", "gx"), "gy"),
        P(("grp", "gx"), "gy"),
        P(None, ("grp", "gx"), "gy"),
        P(None, ("grp", "gx"), "gy"),
    )
    out_specs = (
        P(None, None, ("grp", "gx"), "gy"),
        P(("grp", "gx"), "gy"),
        P(None, ("grp", "gx"), "gy"),
        P(None, ("grp", "gx"), "gy"),
    )
    return jax.shard_map(shards, mesh=mesh, in_specs=in_specs, out_specs=out_specs, check_vma=False)
```

```python
import functools

import jax
import jax.numpy as jnp
from jax import lax
from jax.experimental import pallas as pl
from jax.experimental.pallas import tpu as pltpu
from jax.sharding import PartitionSpec as P

NSUB = 4
CAP = 4
BATCH = 8
MESH = pl.DeviceIdType.MESH


def device_tools(names):
    sizes = {name: lax.axis_size(name) for name in names}
    n_grp, n_gx, n_gy = sizes["grp"], sizes["gx"], sizes["gy"]
    grp, gx, gy = lax.axis_index("grp"), lax.axis_index("gx"), lax.axis_index("gy")
    bx = grp * n_gx + gx

    def at_row(row):
        return (row // n_gx, row % n_gx, gy)

    sides = (
        (bx > 0, at_row(jnp.maximum(bx - 1, 0))),
        (bx < n_grp * n_gx - 1, at_row(jnp.minimum(bx + 1, n_grp * n_gx - 1))),
        (gy > 0, (grp, gx, jnp.maximum(gy - 1, 0))),
        (gy < n_gy - 1, (grp, gx, jnp.minimum(gy + 1, n_gy - 1))),
    )
    return grp, gx, gy, n_grp, n_gx, n_gy, sides


def signal(semaphore, target):
    pl.semaphore_signal(semaphore, inc=1, device_id=target, device_id_type=MESH)


def enter(tools):
    grp, gx, gy, n_grp, n_gx, n_gy, sides = tools
    peers = n_gx * n_gy
    me = gx * n_gy + gy
    barrier = pltpu.get_barrier_semaphore()

    def greet(i, carry):
        peer = lax.rem(me + i, peers)
        signal(barrier, (grp, peer // n_gy, peer % n_gy))
        return carry

    lax.fori_loop(1, peers, greet, 0)
    for i in range(1, n_grp):
        signal(barrier, (lax.rem(grp + i, n_grp), gx, gy))
    cross_low = jnp.logical_and(gx == 0, grp > 0)
    cross_high = jnp.logical_and(gx == n_gx - 1, grp < n_grp - 1)

    @pl.when(cross_low)
    def _():
        signal(barrier, sides[0][1])

    @pl.when(cross_high)
    def _():
        signal(barrier, sides[1][1])

    extra = cross_low.astype(jnp.int32) + cross_high.astype(jnp.int32)
    pl.semaphore_wait(barrier, peers - 1 + n_grp - 1 + extra)


class Gather:
    def __init__(self, tools, source, rows, send_sems, recv_sems):
        self.tools, self.source, self.rows = tools, source, rows
        self.send_sems, self.recv_sems = send_sems, recv_sems
        self.peers = tools[4] * tools[5]
        self.me = tools[1] * tools[5] + tools[2]

    def copy(self, peer, slot):
        n_gy = self.tools[5]
        return pltpu.make_async_remote_copy(
            src_ref=self.source,
            dst_ref=self.rows.at[slot],
            send_sem=self.send_sems.at[peer],
            recv_sem=self.recv_sems.at[slot],
            device_id=(self.tools[0], peer // n_gy, peer % n_gy),
            device_id_type=MESH,
        )

    def start(self, block):
        self.source[...] = block
        self.rows[self.me] = block

        def step(i, carry):
            self.copy(lax.rem(self.me + i, self.peers), self.me).start()
            return carry

        lax.fori_loop(1, self.peers, step, 0)

    def wait(self):
        def step(i, carry):
            peer = lax.rem(self.me + i, self.peers)
            self.copy(peer, peer).wait_recv()
            return carry

        lax.fori_loop(1, self.peers, step, 0)

    def finish(self):
        def step(i, carry):
            peer = lax.rem(self.me + i, self.peers)
            self.copy(peer, peer).wait_send()
            return carry

        lax.fori_loop(1, self.peers, step, 0)


class Rim:
    def __init__(self, tools, source, landing, send_sems, recv_sems):
        self.sides = tools[6]
        self.source, self.landing = source, landing
        self.send_sems, self.recv_sems = send_sems, recv_sems

    def copy(self, side, slot):
        return pltpu.make_async_remote_copy(
            src_ref=self.source.at[side],
            dst_ref=self.landing.at[slot],
            send_sem=self.send_sems.at[side],
            recv_sem=self.recv_sems.at[slot],
            device_id=self.sides[side][1],
            device_id_type=MESH,
        )

    def start(self, side):
        @pl.when(self.sides[side][0])
        def _():
            self.copy(side, side ^ 1).start()

    def wait(self, side):
        @pl.when(self.sides[side][0])
        def _():
            self.copy(side, side).wait_recv()

        @pl.when(jnp.logical_not(self.sides[side][0]))
        def _():
            self.landing[side] = jnp.zeros_like(self.landing[side])

    def finish(self):
        for side in range(4):
            @pl.when(self.sides[side][0])
            def _():
                self.copy(side, side).wait_send()


def stack_rows(rows):
    width = rows[0].shape[1]
    place = lax.broadcasted_iota(jnp.int32, (8, width), 0)
    out = jnp.zeros((8, width), jnp.float32)
    for i, row in enumerate(rows):
        out = jnp.where(place == i, row, out)
    return out


def send_edges(rim, fields):
    last, right = fields[0].shape[0] - 1, fields[0].shape[1] - 1
    rim.source[0] = stack_rows([f[0:1] for f in fields])
    rim.start(0)
    rim.source[1] = stack_rows([f[last:] for f in fields])
    rim.start(1)
    turned = [f.T for f in fields]
    rim.source[2] = stack_rows([f[0:1] for f in turned])
    rim.start(2)
    rim.source[3] = stack_rows([f[right:] for f in turned])
    rim.start(3)


def rim_values(rim, count, shape):
    for side in range(4):
        rim.wait(side)
    row_count, col_count = shape
    line = lax.broadcasted_iota(jnp.int32, (col_count, row_count), 0)
    result = []
    for i in range(count):
        low, high = rim.landing[0, i : i + 1], rim.landing[1, i : i + 1]
        west, east = rim.landing[2, i : i + 1], rim.landing[3, i : i + 1]
        side = jnp.where(line == 0, west, jnp.where(line == col_count - 1, east, 0.0)).T
        result.append((low, high, side))
    return result


def around(field, rim):
    low, high, side = rim
    row_count, col_count = field.shape
    row = lax.broadcasted_iota(jnp.int32, field.shape, 0)
    col = lax.broadcasted_iota(jnp.int32, field.shape, 1)
    return (
        jnp.where(row == row_count - 1, high, pltpu.roll(field, row_count - 1, 0)),
        jnp.where(row == 0, low, pltpu.roll(field, 1, 0)),
        jnp.where(col == col_count - 1, side, pltpu.roll(field, col_count - 1, 1)),
        jnp.where(col == 0, side, pltpu.roll(field, 1, 1)),
    )


def dot(a, b, a_dim, b_dim):
    return lax.dot_general(
        a, b, (((a_dim,), (b_dim,)), ((), ())),
        precision=lax.Precision.HIGHEST, preferred_element_type=jnp.float32,
    )


class Edge:
    def __init__(self, tools, first, sources, landings, send_sems, recv_sems):
        self.sides = tools[6][first : first + 2]
        self.sources, self.landings = sources, landings
        self.send_sems, self.recv_sems = send_sems, recv_sems

    def copy(self, side, slot):
        return pltpu.make_async_remote_copy(
            src_ref=self.sources[side],
            dst_ref=self.landings[slot],
            send_sem=self.send_sems.at[side],
            recv_sem=self.recv_sems.at[slot],
            device_id=self.sides[side][1],
            device_id_type=MESH,
        )

    def start(self):
        for side in range(2):
            @pl.when(self.sides[side][0])
            def _():
                self.copy(side, 1 - side).start()

    def wait(self):
        for side in range(2):
            @pl.when(self.sides[side][0])
            def _():
                self.copy(side, side).wait_recv()

            @pl.when(jnp.logical_not(self.sides[side][0]))
            def _():
                self.landings[side][...] = jnp.zeros(self.landings[side].shape, jnp.float32)

    def finish(self):
        for side in range(2):
            @pl.when(self.sides[side][0])
            def _():
                self.copy(side, side).wait_send()


def row_tiles(layers):
    half = len(layers) // 2
    count = layers[0].shape[0]
    row = lax.broadcasted_iota(jnp.int32, layers[0].shape, 0)
    low, high = [], []
    for a, b in zip(layers[:half], layers[half:]):
        turned = pltpu.roll(b, count // 2, 0)
        low.append(jnp.where(row < count // 2, a, turned))
        high.append(jnp.where(row < count // 2, turned, a))
    return low, high


def halo_tiles(from_low, from_high):
    count = from_low[0].shape[0]
    row = lax.broadcasted_iota(jnp.int32, from_low[0].shape, 0)
    first, second = [], []
    for low, high in zip(from_low, from_high):
        first.append(jnp.where(row < count // 2, high, low))
        second.append(pltpu.roll(jnp.where(row < count // 2, low, high), count // 2, 0))
    return first + second


def packed(layers):
    lane = lax.broadcasted_iota(jnp.int32, layers[0].shape, 1)
    out = jnp.zeros(layers[0].shape, jnp.float32)
    for g, layer in enumerate(layers):
        moved = pltpu.roll(layer, (2 * NSUB * g + NSUB) % layer.shape[1], 1)
        out = jnp.where(lane // (2 * NSUB) == g, moved, out)
    return out


def joined(left, right):
    lane = lax.broadcasted_iota(jnp.int32, left.shape, 1)
    return jnp.where(lane % (2 * NSUB) < NSUB, left, right)


def repeated(pack, slot):
    group = 2 * NSUB
    width = pack.shape[1]
    lane = lax.broadcasted_iota(jnp.int32, pack.shape, 1)
    out = jnp.where(lane // group == slot, pack, 0.0)
    reach = group
    while reach < width:
        out = out + pltpu.roll(out, reach, 1)
        reach *= 2
    return out


def row_ring(pair):
    main, halo = pair
    count = main.shape[0]
    row = lax.broadcasted_iota(jnp.int32, main.shape, 0)
    main_up, halo_up = pltpu.roll(main, count - 1, 0), pltpu.roll(halo, count - 1, 0)
    main_down, halo_down = pltpu.roll(main, 1, 0), pltpu.roll(halo, 1, 0)
    end, begin = row == count - 1, row == 0
    return (
        (jnp.where(end, halo_up, main_up), jnp.where(end, main_up, halo_up)),
        (jnp.where(begin, halo_down, main_down), jnp.where(begin, main_down, halo_down)),
    )


def ring_sides(pair, west=None, east=None):
    width = pair[0].shape[1]
    lane = lax.broadcasted_iota(jnp.int32, pair[0].shape, 1)
    up, down = row_ring(pair)
    right = [pltpu.roll(x, width - 1, 1) for x in pair]
    left = [pltpu.roll(x, 1, 1) for x in pair]
    if west is not None:
        right = [jnp.where(lane == width - 1, e, x) for e, x in zip(east, right)]
        left = [jnp.where(lane == 0, w, x) for w, x in zip(west, left)]
    return up, down, right, left


def ring_weights(mix, wet, mix_ends=(None, None), wet_ends=(None, None)):
    weights = []
    for mix_side, wet_side in zip(ring_sides(mix, *mix_ends), ring_sides(wet, *wet_ends)):
        weights.append([0.5 * (mix[t] + mix_side[t]) * wet[t] * wet_side[t] for t in range(2)])
    stay = [1.0 - (weights[0][t] + weights[1][t] + weights[2][t] + weights[3][t]) for t in range(2)]
    return weights, stay


def spread(pair, weights, west=None, east=None, tiles=2):
    sides, stay = ring_sides(pair, west, east), weights[1]
    out = []
    for t in range(tiles):
        total = stay[t] * pair[t]
        for weight, side in zip(weights[0], sides):
            total = total + weight[t] * side[t]
        out.append(total)
    return out


def spread_rim(pair, weights, rim, tiles):
    width = pair[0].shape[1]
    lane = lax.broadcasted_iota(jnp.int32, pair[0].shape, 1)
    up, down = row_ring(pair)
    out = []
    for t in range(tiles):
        right = pltpu.roll(jnp.where(lane == 0, rim[t], pair[t]), width - 1, 1)
        left = pltpu.roll(jnp.where(lane == width - 1, rim[t], pair[t]), 1, 1)
        rows = weights[0][0][t] * up[t] + weights[0][1][t] * down[t]
        cols = weights[0][2][t] * right + weights[0][3][t] * left
        out.append(weights[1][t] * pair[t] + (rows + cols))
    return out


def column(pair, lane):
    return [x[:, lane : lane + 1] for x in pair]


def surface(fields, moved, cover, draft, tile):
    temp, salt, east, north = [f[tile] for f in fields]
    speed = jnp.sqrt(east * east + north * north + 0.01)
    freezing = -0.5 * salt + 0.3 * draft[tile] - 0.2
    melt = 0.5 * cover[tile] * (temp - freezing) * speed
    drag = 0.05 * cover[tile] * speed
    moved[0][tile] = moved[0][tile] - 0.3 * melt
    moved[1][tile] = moved[1][tile] - 0.2 * melt
    moved[2][tile] = moved[2][tile] - drag * east
    moved[3][tile] = moved[3][tile] - drag * north
    return melt


def slot_table(rows, me, peers, width):
    lane = lax.broadcasted_iota(jnp.int32, (1, width), 1)
    out = jnp.zeros((1, width), jnp.float32)
    for p in range(peers):
        turn = lax.rem(CAP * (p - me) + width, width)
        out = jnp.where(lane // CAP == p, pltpu.roll(rows[p], turn, 1), out)
    return out


def tall(row):
    return jnp.broadcast_to(row, (8, row.shape[1]))


class Ocean:
    def __init__(self, tools, state_ref, next_ref, halo_ref, weight_ref, buffers):
        self.tools, self.state, self.next = tools, state_ref, next_ref
        self.halo, self.weight_ref = halo_ref, weight_ref
        (row_src, row_land, col_src, col_land, row_send, row_recv, col_send, col_recv) = buffers
        self.row_src, self.row_land = row_src, row_land
        self.col_src, self.col_land = col_src, col_land
        self.group = state_ref.shape[2] // (2 * NSUB)
        self.packs = state_ref.shape[0] // self.group
        self.chunks = max(c for c in range(1, 4) if self.packs % c == 0)
        self.each = self.packs // self.chunks
        half = self.group // 2
        self.row_edges, self.col_edges = [], []
        for c in range(self.chunks):
            rows, cols = pl.ds(c * self.each * half, self.each * half), pl.ds(c * self.each, self.each)
            self.row_edges.append(Edge(
                tools, 0, [row_src.at[s, rows] for s in range(2)],
                [row_land.at[s, rows] for s in range(2)], row_send.at[c], row_recv.at[c],
            ))
            self.col_edges.append(Edge(
                tools, 2, [col_src.at[cols]] * 2,
                [col_land.at[s, cols] for s in range(2)], col_send.at[c], col_recv.at[c],
            ))

    def loop(self, c, step):
        def body(v, carry):
            step(v)
            return carry

        lax.fori_loop(c * self.each, (c + 1) * self.each, body, 0)

    def send_rows(self, c):
        half = self.group // 2

        def step(v):
            layers = [self.state[v * self.group + j] for j in range(self.group)]
            low, high = row_tiles(layers)
            for j in range(half):
                self.row_src[0, v * half + j] = low[j]
                self.row_src[1, v * half + j] = high[j]

        self.loop(c, step)
        self.row_edges[c].start()

    def send_columns(self, c):
        half = self.group // 2
        self.row_edges[c].wait()

        def step(v):
            low = [self.row_land[0, v * half + j] for j in range(half)]
            high = [self.row_land[1, v * half + j] for j in range(half)]
            halo = halo_tiles(low, high)
            for j in range(self.group):
                self.halo[v * self.group + j] = halo[j]
            self.col_src[v, 0] = packed([self.state[v * self.group + j] for j in range(self.group)])
            self.col_src[v, 1] = packed(halo)

        self.loop(c, step)
        self.col_edges[c].start()

    def compute(self, c):
        self.col_edges[c].wait()

        def weights_of(block):
            pick = [[self.weight_ref[block, k, t] for t in range(2)] for k in range(5)]
            return pick[:4], pick[4]

        def step(v):
            wings = []
            for block in (0, 2):
                pair = []
                for t in range(2):
                    own = self.col_src[v, t]
                    if block == 0:
                        pair.append(joined(self.col_land[0, v, t], own))
                    else:
                        pair.append(joined(own, self.col_land[1, v, t]))
                stages = [pair]
                weights = weights_of(block)
                for _ in range(NSUB - 1):
                    stages.append(spread(stages[-1], weights))
                wings.append(stages)
            weights = weights_of(1)
            ends = [
                [joined(wings[0][s][t], wings[1][s][t]) for t in range(2)] for s in range(NSUB)
            ]
            width = ends[0][0].shape[1]
            for first in range(0, self.group, BATCH):
                batch = range(first, min(first + BATCH, self.group))
                pairs = [
                    [self.state[v * self.group + j], self.halo[v * self.group + j]] for j in batch
                ]
                for s in range(NSUB):
                    tiles = 1 if s == NSUB - 1 else 2
                    moved = []
                    for j, pair in zip(batch, pairs):
                        turn = (2 * width - NSUB - 2 * NSUB * j) % width
                        rim = [pltpu.roll(ends[s][t], turn, 1) for t in range(tiles)]
                        moved.append(spread_rim(pair, weights, rim, tiles))
                    pairs = moved
                for j, pair in zip(batch, pairs):
                    self.next[v * self.group + j] = pair[0]

        self.loop(c, step)

    def finish(self):
        for edge in self.row_edges + self.col_edges:
            edge.finish()


def top_exchange(tools, layers, src, land, send, recv):
    half = len(layers) // 2
    low, high = row_tiles(layers)
    for j in range(half):
        src[0, j] = low[j]
        src[1, j] = high[j]
    rows = Edge(tools, 0, [src.at[0], src.at[1]], [land.at[0], land.at[1]], send.at[0], recv.at[0])
    rows.start()
    rows.wait()
    halo = halo_tiles([land[0, j] for j in range(half)], [land[1, j] for j in range(half)])
    own = [packed(layers), packed(halo)]
    src[2, 0], src[2, 1] = own
    cols = Edge(
        tools, 2, [src.at[2, pl.ds(0, 2)]] * 2, [land.at[2, pl.ds(0, 2)], land.at[3, pl.ds(0, 2)]],
        send.at[1], recv.at[1],
    )
    cols.start()
    cols.wait()
    west = [joined(land[2, t], own[t]) for t in range(2)]
    east = [joined(own[t], land[3, t]) for t in range(2)]
    blocks = [[[repeated(x, i) for x in west] for i in range(len(layers))]]
    blocks.append([[layers[i], halo[i]] for i in range(len(layers))])
    blocks.append([[repeated(x, i) for x in east] for i in range(len(layers))])
    return blocks, (rows, cols)


def top_steps(blocks, weight_ref, levels, next_ref):
    def ends(i):
        return column(blocks[0][i], NSUB - 1), column(blocks[2][i], NSUB)

    weights = [
        ring_weights(blocks[0][4], blocks[0][5]),
        ring_weights(blocks[1][4], blocks[1][5], ends(4), ends(5)),
        ring_weights(blocks[2][4], blocks[2][5]),
    ]
    for b in range(3):
        for t in range(2):
            for k in range(4):
                weight_ref[b, k, t] = weights[b][0][k][t]
            weight_ref[b, 4, t] = weights[b][1][t]
    fields = [block[:4] for block in blocks]
    total = 0.0
    for s in range(NSUB):
        moved = [[], [], []]
        for i in range(4):
            moved[0].append(spread(fields[0][i], weights[0]))
            west, east = column(fields[0][i], NSUB - 1), column(fields[2][i], NSUB)
            moved[1].append(spread(fields[1][i], weights[1], west, east))
            moved[2].append(spread(fields[2][i], weights[2]))
        for b in range(3):
            for t in range(2):
                melt = surface(fields[b], moved[b], blocks[b][6], blocks[b][7], t)
                if b == 1 and t == 0:
                    total = total + melt
        fields = moved
    return [fields[1][i][0] for i in range(4)], total / NSUB


def step_kernel(
    levels,
    state_hbm,
    mix_ref,
    wet_ref,
    cell_ref,
    slot_ref,
    node_ref,
    thick_hbm,
    visc_hbm,
    fric_hbm,
    ground_hbm,
    coup_hbm,
    drive_hbm,
    guess_hbm,
    next_ref,
    mean_ref,
    vel_ref,
    res_ref,
    state_ref,
    thick_ref,
    visc_ref,
    fric_ref,
    ground_ref,
    coup_ref,
    drive_ref,
    guess_ref,
    load_sems,
    halo_ref,
    weight_ref,
    row_src,
    row_land,
    col_src,
    col_land,
    top_src,
    top_land,
    list_src,
    list_rows,
    sum_src,
    sum_rows,
    half_src,
    half_rows,
    edge_src,
    edge_land,
    row_send,
    row_recv,
    col_send,
    col_recv,
    top_send,
    top_recv,
    list_send,
    list_recv,
    sum_send,
    sum_recv,
    half_send,
    half_recv,
    edge_send,
    edge_recv,
):
    tools = device_tools(("grp", "gx", "gy"))
    grp, gx, gy, n_grp, n_gx, n_gy, sides = tools
    pairs = (
        (thick_hbm, thick_ref),
        (state_hbm, state_ref),
        (visc_hbm, visc_ref),
        (guess_hbm, guess_ref),
        (drive_hbm, drive_ref),
        (fric_hbm, fric_ref),
        (ground_hbm, ground_ref),
        (coup_hbm, coup_ref),
    )
    loads = [pltpu.make_async_copy(a, b, load_sems.at[i]) for i, (a, b) in enumerate(pairs)]
    for load in loads:
        load.start()
    enter(tools)
    me = gx * n_gy + gy
    peers = n_gx * n_gy
    shape = thick_ref.shape
    width = node_ref.shape[1]
    items = cell_ref.shape[1]
    node, cell = node_ref[...], cell_ref[...]
    gathers = [
        Gather(tools, list_src.at[e], list_rows.at[e], list_send.at[e], list_recv.at[e])
        for e in range(2)
    ]
    row_of = (
        lax.broadcasted_iota(jnp.int32, (shape[0], width), 0)
        == jnp.where(node < 0, -1, node // shape[1])
    ).astype(jnp.float32)
    col_of = (lax.broadcasted_iota(jnp.int32, (shape[1], width), 0) == node % shape[1]).astype(jnp.float32)
    loads[0].wait()
    at_node = dot(thick_ref[...].T, row_of, 1, 0)
    gathers[0].start(0.9 * jnp.sum(at_node * col_of, axis=0, keepdims=True))
    ocean = Ocean(
        tools, state_ref, next_ref, halo_ref, weight_ref,
        (row_src, row_land, col_src, col_land, row_send, row_recv, col_send, col_recv),
    )
    loads[1].wait()
    ocean.send_rows(0)
    row_count, col_count = mean_ref.shape
    item_row = (
        lax.broadcasted_iota(jnp.int32, (row_count, items), 0)
        == jnp.where(cell < 0, -1, cell // col_count)
    ).astype(jnp.float32)
    item_col = (lax.broadcasted_iota(jnp.int32, (col_count, items), 0) == cell % col_count).astype(jnp.float32)
    item_slot = (lax.broadcasted_iota(jnp.int32, (width, items), 0) == slot_ref[...]).astype(jnp.float32)
    cover = dot(item_row, item_col, 1, 1)
    gathers[0].wait()
    draft_item = dot(tall(slot_table(list_rows.at[0], me, peers, width)), item_slot, 1, 0)[0:1]
    draft_field = dot(item_row * draft_item, item_col, 1, 1)
    layers = [state_ref[i * levels] for i in range(4)]
    layers += [mix_ref[...], wet_ref[...].astype(jnp.float32), cover, draft_field]
    blocks, top_edges = top_exchange(tools, layers, top_src, top_land, top_send, top_recv)
    top_next, melt_mean = top_steps(blocks, weight_ref, levels, next_ref)
    mean_ref[...] = melt_mean
    melt_item = jnp.sum(dot(melt_mean, item_col, 1, 0) * item_row, axis=0, keepdims=True)
    gathers[1].start(dot(tall(melt_item), item_slot, 1, 1)[0:1])
    for c in range(1, ocean.chunks):
        ocean.send_rows(c)
    for load in loads[2:]:
        load.wait()
    friction = fric_ref[...] * ground_ref[...].astype(jnp.float32) + 0.2
    cross = 0.9 * friction * coup_ref[...]
    ocean.send_columns(0)
    gathers[1].wait()
    melt = slot_table(list_rows.at[1], me, peers, width)
    melt_node = dot(row_of * melt, col_of, 1, 1)
    thinned = thick_ref[...] * jnp.exp(-0.3 * melt_node)
    depth_visc = visc_ref[...] * thinned
    guess = [guess_ref[0], guess_ref[1]]
    rims = [Rim(tools, edge_src.at[e], edge_land.at[e], edge_send.at[e], edge_recv.at[e]) for e in range(3)]
    send_edges(rims[0], [depth_visc] + guess)
    ocean.compute(0)
    values = rim_values(rims[0], 3, shape)
    weights = [0.5 * (depth_visc + beside) for beside in around(depth_visc, values[0])]
    diagonal = weights[0] + weights[1] + weights[2] + weights[3] + friction
    scale = 1.0 / diagonal

    def apply(vector, rim):
        out = []
        for i in range(2):
            beside = 0.0
            for weight, side in zip(weights, around(vector[i], rim[i])):
                beside = beside + weight * side
            out.append(diagonal * vector[i] - beside + cross * vector[1 - i])
        return out

    def half_sums(index, products):
        rows = [jnp.sum(a[0] * b[0] + a[1] * b[1], axis=0, keepdims=True) for a, b in products]
        part = Gather(tools, sum_src.at[index], sum_rows.at[index], sum_send.at[index], sum_recv.at[index])
        part.start(stack_rows(rows))
        return part

    def whole_sums(index, part, count):
        part.wait()
        total = jnp.sum(sum_rows[index], axis=0)
        half_src[index] = total
        copies = []
        for i in range(1, n_grp):
            copies.append(pltpu.make_async_remote_copy(
                src_ref=half_src.at[index], dst_ref=half_rows.at[index, i - 1],
                send_sem=half_send.at[index, i - 1], recv_sem=half_recv.at[index, i - 1],
                device_id=(lax.rem(grp + i, n_grp), gx, gy), device_id_type=MESH,
            ))
            copies[-1].start()
        for i, copy in enumerate(copies):
            copy.wait()
            total = total + half_rows[index, i]
        summed = jnp.sum(total, axis=1, keepdims=True)
        return [summed[i : i + 1] for i in range(count)]

    image = apply(guess, values[1:])
    residual = [drive_ref[i] * thinned - image[i] for i in range(2)]
    precond = [residual[i] * scale for i in range(2)]
    send_edges(rims[1], precond)
    if ocean.chunks > 1:
        ocean.send_columns(1)
    edge_z = rim_values(rims[1], 2, shape)
    image = apply(precond, edge_z)
    scaled = [image[i] * scale for i in range(2)]
    part = half_sums(0, [(residual, precond), (precond, image)])
    send_edges(rims[2], scaled)
    for c in range(2, ocean.chunks):
        ocean.send_columns(c)
    edge_y = rim_values(rims[2], 2, shape)
    if ocean.chunks > 1:
        ocean.compute(1)
    norm, curve = whole_sums(0, part, 2)
    step = norm / curve
    velocity = [guess[i] + step * precond[i] for i in range(2)]
    residual = [residual[i] - step * image[i] for i in range(2)]
    next_precond = [residual[i] * scale for i in range(2)]
    edge = [tuple(z - step * y for z, y in zip(edge_z[i], edge_y[i])) for i in range(2)]
    next_image = apply(next_precond, edge)
    second = half_sums(1, [(residual, next_precond), (next_precond, next_image), (next_precond, image)])
    for c in range(2, ocean.chunks):
        ocean.compute(c)
    norm_next, own_curve, mixed = whole_sums(1, second, 3)
    ratio = norm_next / norm
    step = norm_next / (own_curve + 2.0 * ratio * mixed + ratio * ratio * curve)
    for i in range(2):
        vel_ref[i] = velocity[i] + step * (next_precond[i] + ratio * precond[i])
        res_ref[i] = residual[i] - step * (next_image[i] + ratio * image[i])
    for i in range(4):
        next_ref[i * levels] = top_next[i]
    ocean.finish()
    for edge in top_edges:
        edge.finish()
    for gather in gathers:
        gather.finish()
    part.finish()
    second.finish()
    for rim in rims:
        rim.finish()


def whole_step(arrays, levels):
    n_grp, n_gx, n_gy = lax.axis_size("grp"), lax.axis_size("gx"), lax.axis_size("gy")
    peers = n_gx * n_gy
    state, mix, guess = arrays[0], arrays[1], arrays[12]
    width, cols = arrays[5].shape[1], guess.shape[2]
    layer_total, row_count, col_count = state.shape
    group = col_count // (2 * NSUB)
    packs = layer_total // group
    vmem = pl.BlockSpec(memory_space=pltpu.VMEM)
    hbm = pl.BlockSpec(memory_space=pltpu.HBM)
    dma = pltpu.SemaphoreType.DMA
    f32 = jnp.float32

    def buffer(*dims):
        return pltpu.VMEM(dims, f32)

    tile = (row_count, col_count)
    return pl.pallas_call(
        functools.partial(step_kernel, levels),
        out_shape=[jax.ShapeDtypeStruct(a.shape, f32) for a in (state, mix, guess, guess)],
        in_specs=[hbm, vmem, vmem, vmem, vmem, vmem] + [hbm] * 7,
        out_specs=[vmem] * 4,
        scratch_shapes=[
            *(pltpu.VMEM(arrays[i].shape, arrays[i].dtype) for i in (0, 6, 7, 8, 9, 10, 11, 12)),
            dma((8,)),
            buffer(layer_total, *tile),
            buffer(3, 5, 2, *tile),
            buffer(2, layer_total // 2, *tile),
            buffer(2, layer_total // 2, *tile),
            buffer(packs, 2, *tile),
            buffer(2, packs, 2, *tile),
            buffer(3, 4, *tile),
            buffer(4, 4, *tile),
            buffer(2, 1, width),
            buffer(2, peers, 1, width),
            buffer(2, 8, cols),
            buffer(2, peers, 8, cols),
            buffer(2, 8, cols),
            buffer(2, n_grp - 1, 8, cols),
            buffer(3, 4, 8, cols),
            buffer(3, 4, 8, cols),
            dma((3, 2)),
            dma((3, 2)),
            dma((3, 2)),
            dma((3, 2)),
            dma((2, 2)),
            dma((2, 2)),
            dma((2, peers)),
            dma((2, peers)),
            dma((2, peers)),
            dma((2, peers)),
            dma((2, n_grp - 1)),
            dma((2, n_grp - 1)),
            dma((3, 4)),
            dma((3, 4)),
        ],
        compiler_params=pltpu.CompilerParams(
            collective_id=0, has_side_effects=True, vmem_limit_bytes=56 * 1024 * 1024
        ),
    )(*arrays)


def shards(
    ocean_state,
    diffusivity,
    wet_mask,
    coast_column,
    coast_slot,
    owner_node,
    thickness,
    viscosity,
    friction,
    grounded,
    coupling,
    driving,
    first_guess,
):
    field_count, level_count, row_count, col_count = ocean_state.shape

    def lane_row(values):
        flat = values.reshape(1, -1)
        return jnp.pad(flat, ((0, 0), (0, -flat.shape[1] % 128)), constant_values=-1)

    fields, melt_mean, velocity, residual = whole_step(
        (
            ocean_state.reshape(-1, row_count, col_count),
            diffusivity,
            wet_mask,
            lane_row(coast_column),
            lane_row(coast_slot),
            lane_row(owner_node),
            thickness,
            viscosity,
            friction,
            grounded,
            coupling,
            driving,
            first_guess,
        ),
        level_count,
    )
    return (fields.reshape(ocean_state.shape), melt_mean, velocity, residual)


def solution(mesh):
    in_specs = (
        P(None, None, ("grp", "gx"), "gy"),
        P(("grp", "gx"), "gy"),
        P(("grp", "gx"), "gy"),
        P(("grp", "gx"), "gy", None),
        P(("grp", "gx"), "gy", None),
        P(("grp", "gx"), "gy", None, None),
        P(("grp", "gx"), "gy"),
        P(("grp", "gx"), "gy"),
        P(("grp", "gx"), "gy"),
        P(("grp", "gx"), "gy"),
        P(("grp", "gx"), "gy"),
        P(None, ("grp", "gx"), "gy"),
        P(None, ("grp", "gx"), "gy"),
    )
    out_specs = (
        P(None, None, ("grp", "gx"), "gy"),
        P(("grp", "gx"), "gy"),
        P(None, ("grp", "gx"), "gy"),
        P(None, ("grp", "gx"), "gy"),
    )
    return jax.shard_map(shards, mesh=mesh, in_specs=in_specs, out_specs=out_specs, check_vma=False)
```
